256 devices in a mesh: dp: 4 (over x), expert: 4 (over y), tensor: 16 (over z, core).
Axes of the slice: x: 4, y: 4, z: 8, core: 2. Of those that a mesh axis runs over, the one named last changes fastest.
Arguments:
- mixer_input: bfloat16 [128, 4, 8192], P(('dp', 'expert'), None, 'tensor'), may hold values from -6 to 6
- gating_input: bfloat16 [128, 4, 8192], P(('dp', 'expert'), None, 'tensor'), may hold values from -6 to 6
- conv_cache: bfloat16 [128, 3, 8192], P(('dp', 'expert'), None, 'tensor'), may hold values from -6 to 6
- conv_weight: bfloat16 [4, 8192], P(None, 'tensor'), may hold values from -3 to 3
- conv_bias: float32 [8192], P('tensor'), may hold values from -3 to 3
- ssm_state: float32 [128, 16, 8192], P(('dp', 'expert'), None, 'tensor'), may hold values from -3 to 3
- xproj_codes: bfloat16 [8192, 544], P('tensor'), may hold values from -7.5 to 7.5, as said below
- xproj_scale: int32 [544], replicated, may hold values from 32 to 127
- dtproj_codes: bfloat16 [512, 8192], P(None, 'tensor'), may hold values from -7.5 to 7.5, as said below
- dtproj_scale: int32 [8192], P('tensor'), may hold values from 32 to 127
- step_bias: float32 [8192], P('tensor'), may hold values from -4 to 0
- decay_log: float32 [16, 8192], P(None, 'tensor'), may hold values from 0 to 2.77
- skip_gain: float32 [8192], P('tensor'), may hold values from 0.5 to 1.5
- outproj_codes: bfloat16 [16, 4, 128, 8192], P('tensor', 'expert'), may hold values from -7.5 to 7.5, as said below
- outproj_scale: int32 [8192], replicated, may hold values from 32 to 127
- residual: bfloat16 [128, 4, 8192], P('dp', None, ('expert', 'tensor')), may hold values from -6 to 6
- norm_gain: float32 [8192], replicated, may hold values from 0.1 to 1.9
- expert_ids: int32 [128, 4, 2], P('dp'), may hold values from 0 to 3, all different within a row; in each aligned block of 128 rows (0 to 127, 128 to 255, ..., all dimensions but the last counted through in order) at most 96 rows name the same one
- expert_gates: float32 [128, 4, 2], P('dp'), may hold values from 0.2 to 1
- gate_codes: bfloat16 [4, 8192, 12288], P('expert', None, ('dp', 'tensor')), may hold values from -7.5 to 7.5, as said below
- up_codes: bfloat16 [4, 8192, 12288], P('expert', None, ('dp', 'tensor')), may hold values from -7.5 to 7.5, as said below
- down_codes: bfloat16 [4, 12288, 8192], P('expert', ('dp', 'tensor')), may hold values from -7.5 to 7.5, as said below
- gate_scale: int32 [4, 12288], P('expert', ('dp', 'tensor')), may hold values from 32 to 127
- up_scale: int32 [4, 12288], P('expert', ('dp', 'tensor')), may hold values from 32 to 127
- down_scale: int32 [4, 8192], P('expert'), may hold values from 32 to 127
Outputs:
- layer_out: bfloat16 [128, 4, 8192], P('dp', None, ('expert', 'tensor'))
- new_state: float32 [128, 16, 8192], P(('dp', 'expert'), None, 'tensor')
The draws below stay inside these ranges and needn't reach their ends.
Inputs may be any that keep to these rules, and one draw needn't show every extreme that they name: `expert_ids`: each token names 2 different experts. Among the 128 tokens of one dp index, no expert is named by more than 96 tokens, and in some dp indices one expert is named by exactly 96. `xproj_codes`: every entry is an integer of 0 to 15 minus 7.5. `dtproj_codes`: every entry is an integer of 0 to 15 minus 7.5. `outproj_codes`: every entry is an integer of 0 to 15 minus 7.5. `gate_codes`: every entry is an integer of 0 to 15 minus 7.5. `up_codes`: every entry is an integer of 0 to 15 minus 7.5. `down_codes`: every entry is an integer of 0 to 15 minus 7.5.
All inputs are finite; a program needn't handle non-finite values.
Results may differ from the reference program's by a relative error of at most 0.019.
Values may be sent and summed in bfloat16 or wider, within the bound.
No kernel may reach another device: no remote copies, remote signals or barrier semaphores. Data moves between devices by JAX's collectives and lax.ppermute only.
A program may use at most 128 MiB of HBM per device.

```python
import math
import jax
import jax.numpy as jnp
import numpy as np
from jax import lax

D = 8192
INNER = 8192
NSTATE = 16
DTR = 512
CONV = 4
TOP = 2
FF = 12288
STEPS = 4
ROWS_DP = 32
EXPERTS = 4
ROWS = 128
TOKENS = 512
TOKG = 128
CAP = 96
HBLOCK = 512
XW = 544
SLAB = 512
SUB = 128


def level_table(key, shape):
    return jax.random.randint(key, shape, 0, 16).astype(jnp.float32) - 7.5


def draw_xproj_codes(key, part):
    key = jax.random.fold_in(key, 11)
    return level_table(key, (INNER, XW)).astype(jnp.bfloat16)


def draw_dtproj_codes(key, part):
    key = jax.random.fold_in(key, 12)
    return level_table(key, (DTR, INNER)).astype(jnp.bfloat16)


def draw_outproj_codes(key, part):
    key = jax.random.fold_in(key, 13)
    return level_table(key, (INNER // SLAB, SLAB // SUB, SUB, D)).astype(jnp.bfloat16)


def draw_gate_codes(key, part):
    key = jax.random.fold_in(key, 14)
    return level_table(key, (EXPERTS, D, FF)).astype(jnp.bfloat16)


def draw_up_codes(key, part):
    key = jax.random.fold_in(key, 15)
    return level_table(key, (EXPERTS, D, FF)).astype(jnp.bfloat16)


def draw_down_codes(key, part):
    key = jax.random.fold_in(key, 16)
    return level_table(key, (EXPERTS, FF, D)).astype(jnp.bfloat16)


def with_ends(entries, key, low, high):
    spot = [jax.random.randint(jax.random.fold_in(key, axis), (), 0, length) for axis, length in enumerate(entries.shape)]
    longest = entries.shape.index(max(entries.shape))
    next_to = spot[:longest] + [(spot[longest] + 1) % entries.shape[longest]] + spot[longest + 1:]
    return entries.at[tuple(spot)].set(low).at[tuple(next_to)].set(high)


def block_scale(rng, shape, cuts, low, top_value):
    def one(axis_at, shards_of):
        draws = jax.random.uniform(jax.random.fold_in(jax.random.fold_in(rng, 6), axis_at), (shards_of,), jnp.float32, low / len(cuts), top_value / len(cuts))
        return jnp.repeat(jnp.exp(draws), shape[axis_at] // shards_of).reshape((-1,) + (1,) * (len(shape) - axis_at - 1))

    gain = one(*cuts[0])
    for cut in cuts[1:]:
        gain = gain * one(*cut)
    return gain


def assign_block(rng, own, number, rows, amount, top, most, lean):
    ranking = jax.random.permutation(rng, amount)
    heavy_load, ordinary = load_shares(amount, rows * top, most, lean, True), load_shares(amount, rows * top, most, lean, False)
    places = jnp.arange(amount)

    def named(lengths, turn):
        used = int((lengths > 0).sum())
        fixed = max(1, used // 4)
        moved = fixed + (places - fixed + turn * (used - fixed)) % max(1, amount - fixed)
        return jnp.zeros((amount,), jnp.int32).at[ranking[jnp.where(places < fixed, places, moved)]].set(jnp.asarray(lengths, jnp.int32))

    lengths = jnp.where(number % 4 == 0, named(heavy_load, number // 4), named(ordinary, number - number // 4 - 1))
    mixed = jax.random.permutation(jax.random.fold_in(own, 3), amount)
    giver, receiver = mixed[0:amount // 2 * 2:2], mixed[1:amount // 2 * 2:2]
    margin = jnp.minimum(lengths[giver] - 1, most - lengths[receiver]) // 2
    margin = jnp.where((giver == ranking[0]) | (receiver == ranking[0]) | (lengths[receiver] == 0), 0, jnp.maximum(margin, 0))
    moved = jax.random.randint(jax.random.fold_in(own, 4), (amount // 2,), 0, 1 << 20) % (margin + 1)
    lengths = lengths.at[giver].add(-moved).at[receiver].add(moved)
    members = jnp.searchsorted(jnp.cumsum(lengths), jnp.arange(rows * top), side="right").astype(jnp.int32)
    grid = members.reshape(top, rows).T
    grid = grid[jax.random.permutation(jax.random.fold_in(own, 1), rows)]
    turn = jax.random.randint(jax.random.fold_in(own, 2), (rows, 1), 0, top)
    return jnp.take_along_axis(grid, (jnp.arange(top)[None, :] + turn) % top, axis=1)


def load_shares(number_of, total, reach, slope, full):
    portions = [(1 << 20) // math.isqrt(rank ** slope) + 1 for rank in range(1, number_of + 1)]
    largest = reach if full else min(reach, max(-(-total // number_of), total * portions[0] // sum(portions)))
    least = 1 if total - largest >= number_of - 1 else 0
    given, spare = [largest] + [least] * (number_of - 1), total - largest - least * (number_of - 1)
    while spare > 0:
        movable = [i for i in range(1, number_of) if given[i] < largest] or [i for i in range(1, number_of) if given[i] < reach]
        mass, left = sum([portions[i] for i in movable]), spare
        for i in movable:
            addition = min(reach - given[i], max(1, left * portions[i] // mass), spare)
            given[i] = given[i] + addition
            spare = spare - addition
    return np.array(given)


def scatter_about(stream_key, shape, deviation, bound, split=(), kind=jnp.bfloat16):
    drawn = deviation * jax.random.normal(stream_key, shape, jnp.float32)
    if split:
        drawn = drawn * block_scale(stream_key, shape, split, -0.22, 0.18)
    return jnp.clip(drawn, -bound, bound).astype(kind)


def setup_inputs(seed: int = 0) -> dict:
    streams_of = jax.random.split(jax.random.key(seed), 26)
    mixer_input = scatter_about(streams_of[0], (ROWS, STEPS, INNER), 1.0, 6.0, ((0, 16), (2, 16)))
    gating_input = scatter_about(streams_of[1], (ROWS, STEPS, INNER), 1.0, 6.0, ((0, 16), (2, 16)))
    conv_cache = scatter_about(streams_of[2], (ROWS, CONV - 1, INNER), 1.0, 6.0, ((0, 16), (2, 16)))
    conv_weight = scatter_about(streams_of[3], (CONV, INNER), CONV ** -0.5, 3.0, ((1, 16),))
    conv_bias = scatter_about(streams_of[4], (INNER,), 0.5, 3.0, ((0, 16),), jnp.float32)
    ssm_state = scatter_about(streams_of[5], (ROWS, NSTATE, INNER), 0.5, 3.0, ((0, 16), (2, 16)), jnp.float32)
    xproj_codes = draw_xproj_codes(jax.random.fold_in(streams_of[25], 71), 0)
    xproj_scale = with_ends(jax.random.randint(streams_of[7], (XW,), 32, 128), jax.random.fold_in(streams_of[7], 1), 32, 127).astype(jnp.int32)
    dtproj_codes = draw_dtproj_codes(jax.random.fold_in(streams_of[25], 71), 0)
    dtproj_scale = with_ends(jax.random.randint(streams_of[9], (INNER,), 32, 128), jax.random.fold_in(streams_of[9], 1), 32, 127).astype(jnp.int32)
    step_bias = jnp.clip(-4.0 + 4.0 * jax.random.uniform(streams_of[10], (INNER,), jnp.float32) ** block_scale(streams_of[10], (INNER,), ((0, 16),), -0.2, 0.2), -4.0, 0.0)
    decay_log = jnp.clip(2.77 * jax.random.uniform(streams_of[11], (NSTATE, INNER), jnp.float32) ** block_scale(streams_of[11], (NSTATE, INNER), ((1, 16),), -0.2, 0.2), 0.0, 2.77)
    skip_gain = jnp.clip(0.5 + 1.0 * jax.random.uniform(streams_of[12], (INNER,), jnp.float32) ** block_scale(streams_of[12], (INNER,), ((0, 16),), -0.2, 0.2), 0.5, 1.5)
    outproj_codes = draw_outproj_codes(jax.random.fold_in(streams_of[25], 71), 0)
    outproj_scale = with_ends(jax.random.randint(streams_of[14], (D,), 32, 128), jax.random.fold_in(streams_of[14], 1), 32, 127).astype(jnp.int32)
    residual = scatter_about(streams_of[15], (ROWS, STEPS, D), 1.0, 6.0, ((0, 4), (2, 64)))
    norm_gain = jnp.clip(1.0 + 0.18 * jax.random.normal(streams_of[16], (D,), jnp.float32), 0.1, 1.9)
    expert_ids_keys = jax.random.split(jax.random.fold_in(streams_of[17], 1), ROWS * STEPS // TOKG)
    expert_ids_turns = jax.random.permutation(jax.random.fold_in(streams_of[17], 3), ROWS * STEPS // TOKG)
    expert_ids = jax.vmap(lambda own, number: assign_block(jax.random.fold_in(streams_of[17], 2), own, number, TOKG, EXPERTS, TOP, CAP, 1))(expert_ids_keys, expert_ids_turns).reshape((ROWS, STEPS, TOP))
    expert_gates = jnp.clip(0.2 + 0.8 * jax.random.uniform(streams_of[18], (ROWS, STEPS, TOP), jnp.float32) ** block_scale(streams_of[18], (ROWS, STEPS, TOP), ((0, 4),), -0.2, 0.2), 0.2, 1.0)
    gate_codes = draw_gate_codes(jax.random.fold_in(streams_of[25], 71), 0)
    up_codes = draw_up_codes(jax.random.fold_in(streams_of[25], 71), 0)
    down_codes = draw_down_codes(jax.random.fold_in(streams_of[25], 71), 0)
    gate_scale = with_ends(jax.random.randint(streams_of[22], (EXPERTS, FF), 32, 128), jax.random.fold_in(streams_of[22], 1), 32, 127).astype(jnp.int32)
    up_scale = with_ends(jax.random.randint(streams_of[23], (EXPERTS, FF), 32, 128), jax.random.fold_in(streams_of[23], 1), 32, 127).astype(jnp.int32)
    down_scale = with_ends(jax.random.randint(streams_of[24], (EXPERTS, D), 32, 128), jax.random.fold_in(streams_of[24], 1), 32, 127).astype(jnp.int32)
    return dict(mixer_input=mixer_input, gating_input=gating_input, conv_cache=conv_cache, conv_weight=conv_weight, conv_bias=conv_bias, ssm_state=ssm_state, xproj_codes=xproj_codes, xproj_scale=xproj_scale, dtproj_codes=dtproj_codes, dtproj_scale=dtproj_scale, step_bias=step_bias, decay_log=decay_log, skip_gain=skip_gain, outproj_codes=outproj_codes, outproj_scale=outproj_scale, residual=residual, norm_gain=norm_gain, expert_ids=expert_ids, expert_gates=expert_gates, gate_codes=gate_codes, up_codes=up_codes, down_codes=down_codes, gate_scale=gate_scale, up_scale=up_scale, down_scale=down_scale)


def sign_table(left, right, size):
    both = jnp.bitwise_and(left, right)
    parity = jnp.zeros_like(both)
    for level in range(size.bit_length() - 1):
        parity = jnp.bitwise_xor(parity, jnp.bitwise_and(jnp.right_shift(both, level), 1))
    return (1 - 2 * parity).astype(jnp.float32)

def sylvester(size):
    index = jnp.arange(size, dtype=jnp.int32)
    return sign_table(index[:, None], index[None, :], size)

def column_factor(scale, fan_in):
    return scale.astype(jnp.float32) / (368.0 * math.sqrt(fan_in))

def quant_dot(left, table, factor):
    return jnp.dot(left, table, preferred_element_type=jnp.float32) * factor

def reference(mixer_input, gating_input, conv_cache, conv_weight, conv_bias, ssm_state, xproj_codes, xproj_scale, dtproj_codes, dtproj_scale, step_bias, decay_log, skip_gain, outproj_codes, outproj_scale, residual, norm_gain, expert_ids, expert_gates, gate_codes, up_codes, down_codes, gate_scale, up_scale, down_scale):
    highest = lax.Precision.HIGHEST
    window = jnp.concatenate([conv_cache, mixer_input], axis=1).astype(jnp.float32)
    kernel = conv_weight.astype(jnp.float32)
    convolved = conv_bias + sum((kernel[shift] * window[:, shift:shift + STEPS] for shift in range(CONV)))
    activated = jax.nn.silu(convolved)
    inner_bf = activated.astype(jnp.bfloat16).reshape(TOKENS, INNER)
    projected = quant_dot(inner_bf, xproj_codes, column_factor(xproj_scale, INNER))
    low_rank = projected[:, :DTR].astype(jnp.bfloat16)
    input_coef = projected[:, DTR:DTR + NSTATE].reshape(ROWS, STEPS, NSTATE)
    output_coef = projected[:, DTR + NSTATE:].reshape(ROWS, STEPS, NSTATE)
    step_size = jax.nn.softplus(quant_dot(low_rank, dtproj_codes, column_factor(dtproj_scale, DTR)) + step_bias).reshape(ROWS, STEPS, INNER)
    decay_rate = -jnp.exp(decay_log)
    gate_act = jax.nn.silu(gating_input.astype(jnp.float32))
    state = ssm_state
    outputs = []
    for moment in range(STEPS):
        delta = step_size[:, moment]
        current = activated[:, moment]
        state = jnp.exp(delta[:, None, :] * decay_rate[None]) * state + (delta * current)[:, None, :] * input_coef[:, moment][:, :, None]
        readout = lax.optimization_barrier(jnp.sum(output_coef[:, moment][:, :, None] * state, axis=1)) + skip_gain * current
        outputs.append((readout * gate_act[:, moment]).astype(jnp.bfloat16))
    gated = jnp.stack(outputs, axis=1)
    rotated = jnp.dot(gated.reshape(TOKENS * 16, HBLOCK), sylvester(HBLOCK).astype(jnp.bfloat16), preferred_element_type=jnp.float32)
    rotated = rotated.astype(jnp.bfloat16).reshape(TOKENS, 16, HBLOCK)
    mixed = jnp.einsum('ab,tbk->tak', sylvester(16), rotated.astype(jnp.float32), precision=highest)
    mixed_bf = (mixed * (1.0 / math.sqrt(INNER))).astype(jnp.bfloat16).reshape(TOKENS, INNER)
    block_out = quant_dot(mixed_bf, outproj_codes.reshape(INNER, D), column_factor(outproj_scale, INNER))
    hidden = (residual.reshape(TOKENS, D).astype(jnp.float32) + block_out).astype(jnp.bfloat16)
    values = hidden.astype(jnp.float32)
    mean_square = lax.optimization_barrier(jnp.mean(values * values, axis=-1, keepdims=True))
    normed = (values * lax.rsqrt(mean_square + 1e-05) * norm_gain).astype(jnp.bfloat16)
    groups = ROWS // ROWS_DP
    route = expert_ids.reshape(groups, TOKG, TOP)
    gate_values = expert_gates.reshape(groups, TOKG, TOP)
    normed_groups = normed.reshape(groups, TOKG, D).astype(jnp.float32)
    slots = jnp.arange(CAP, dtype=jnp.int32)

    def one_expert(operands):
        index, gate_table, up_table, down_table, gate_col, up_col, down_col = operands
        hit = route == index
        member = jnp.any(hit, axis=-1).astype(jnp.int32)
        token_weight = lax.optimization_barrier(jnp.sum(jnp.where(hit, gate_values, 0.0), axis=-1))
        position = jnp.cumsum(member, axis=-1, dtype=jnp.int32) - 1
        onehot = ((position[:, None, :] == slots[None, :, None]) & (member[:, None, :] == 1)).astype(jnp.float32)
        slot_input = jnp.einsum('gst,gtd->gsd', onehot, normed_groups, precision=highest).astype(jnp.bfloat16).reshape(groups * CAP, D)
        gate_part = quant_dot(slot_input, gate_table, column_factor(gate_col, D))
        up_part = quant_dot(slot_input, up_table, column_factor(up_col, D))
        expert_hidden = (jax.nn.silu(gate_part) * up_part).astype(jnp.bfloat16)
        expert_out = quant_dot(expert_hidden, down_table, column_factor(down_col, FF)).reshape(groups, CAP, D)
        slot_weight = jnp.einsum('gst,gt->gs', onehot, token_weight, precision=highest)
        return jnp.einsum('gst,gsd->gtd', onehot, expert_out * slot_weight[:, :, None], precision=highest)
    per_expert = lax.map(one_expert, (jnp.arange(EXPERTS, dtype=jnp.int32), gate_codes, up_codes, down_codes, gate_scale, up_scale, down_scale))
    moe = lax.optimization_barrier(jnp.sum(per_expert, axis=0)).reshape(TOKENS, D)
    layer_out = (hidden.astype(jnp.float32) + moe).astype(jnp.bfloat16).reshape(ROWS, STEPS, D)
    return (layer_out, state)
```

```python
import math

import jax
import jax.numpy as jnp
from jax import lax
from jax.experimental import pallas as pl
from jax.experimental.pallas import tpu as pltpu
from jax.sharding import PartitionSpec as P

BF = jnp.bfloat16
F32 = jnp.float32
LEVEL = 368.0
VMEM_BYTES = 50 * 1024 * 1024


def sign_table(left, right, size):
    both = jnp.bitwise_and(left, right)
    parity = jnp.zeros_like(both)
    for level in range(size.bit_length() - 1):
        parity = jnp.bitwise_xor(parity, jnp.bitwise_and(jnp.right_shift(both, level), 1))
    return (1 - 2 * parity).astype(F32)


def dot(a, b):
    return jnp.dot(a, b, preferred_element_type=F32)


def silu(x):
    return x * (1.0 / (1.0 + jnp.exp(-x)))


def shift_z(a, k):
    pairs = [(z * 2 + c, ((z + k) % 8) * 2 + c) for z in range(8) for c in range(2)]
    return lax.ppermute(a, "tensor", pairs)


def swap_core(a):
    return lax.ppermute(a, "tensor", [(t, t ^ 1) for t in range(16)])


def shift_x(a, k):
    return lax.ppermute(a, "dp", [(i, (i + k) % 4) for i in range(4)])


def shift_y(a, k):
    return lax.ppermute(a, "expert", [(i, (i + k) % 4) for i in range(4)])


def call(kernel, outs, operands, scalars=0, scratch=(), flops=0, moved=0):
    vmem = pl.BlockSpec(memory_space=pltpu.VMEM)
    smem = pl.BlockSpec(memory_space=pltpu.SMEM)
    specs = [smem] * scalars + [vmem] * (len(operands) - scalars)
    return pl.pallas_call(
        kernel,
        out_shape=outs,
        in_specs=specs,
        out_specs=jax.tree.map(lambda _: vmem, outs),
        scratch_shapes=list(scratch),
        compiler_params=pltpu.CompilerParams(vmem_limit_bytes=VMEM_BYTES),
        cost_estimate=pl.CostEstimate(flops=flops, bytes_accessed=moved, transcendentals=0),
    )(*operands)


def conv_kernel(mix_ref, cache_ref, taps_ref, bias_ref, table_ref, scale_ref, act_ref, part_ref):
    steps = mix_ref.shape[1]
    inner = 16 * mix_ref.shape[2]
    mix = mix_ref[...].astype(F32)
    cache = cache_ref[...].astype(F32)
    window = [cache[:, k, :] for k in range(cache.shape[1])] + [mix[:, k, :] for k in range(steps)]
    taps = taps_ref[...].astype(F32)
    acts = []
    for t in range(steps):
        total = bias_ref[...]
        for k in range(taps.shape[0]):
            total = total + taps[k : k + 1, :] * window[t + k]
        act = silu(total)
        act_ref[t] = act
        acts.append(act)
    flat = jnp.concatenate(acts, axis=0).astype(BF)
    factor = scale_ref[...].astype(F32) / (LEVEL * math.sqrt(inner))
    part_ref[...] = dot(flat, table_ref[...]) * factor


def scan_kernel(
    q_ref, p_ref, m_ref, a_ref, b_ref, table_ref, scale_ref, bias_ref, decay_ref, act_ref,
    gate_ref, skip_ref, state_ref, had_ref, rot_ref, new_ref, delta_ref, read_ref,
):
    rank = table_ref.shape[0]
    nstate = decay_ref.shape[0]
    rows, steps = gate_ref.shape[0], gate_ref.shape[1]
    proj = q_ref[...] + p_ref[...].astype(F32) + m_ref[...].astype(F32)
    proj = proj + a_ref[...].astype(F32) + b_ref[...].astype(F32)
    factor = scale_ref[...].astype(F32) / (LEVEL * math.sqrt(rank))
    pre = dot(proj[:, :rank].astype(BF), table_ref[...]) * factor + bias_ref[...]
    delta_ref[...] = jnp.maximum(pre, 0.0) + jnp.log1p(jnp.exp(-jnp.abs(pre)))
    coef = jnp.transpose(proj[:, rank:])
    decay = -jnp.exp(decay_ref[...])
    for r in range(rows):
        state = state_ref[r]
        for t in range(steps):
            row = t * rows + r
            delta = delta_ref[row : row + 1, :]
            current = act_ref[t, r : r + 1, :]
            into = coef[0:nstate, row : row + 1]
            out = coef[nstate : 2 * nstate, row : row + 1]
            state = jnp.exp(delta * decay) * state + (delta * current) * into
            read_ref[row : row + 1, :] = jnp.sum(out * state, axis=0, keepdims=True)
        new_ref[r] = state
    gate = gate_ref[...].astype(F32)
    gated = []
    for t in range(steps):
        readout = read_ref[t * rows : (t + 1) * rows, :] + skip_ref[...] * act_ref[t]
        gated.append(readout * silu(gate[:, t, :]))
    gated = jnp.concatenate(gated, axis=0).astype(BF)
    rot_ref[...] = dot(gated, had_ref[...]).astype(BF)


def out_kernel(
    sign_ref, place_ref, own_ref, m_ref, p_ref, far_ref, back_ref,
    w0_ref, w1_ref, w2a_ref, w2b_ref, w3_ref, scale_ref, mine_ref, other_ref,
):
    rows = own_ref.shape[0]
    inner = 16 * own_ref.shape[1]
    pieces = [own_ref[...], m_ref[...]]
    pieces += [far_ref[i * rows : (i + 1) * rows] for i in range(3)]
    pieces += [back_ref[i * rows : (i + 1) * rows] for i in range(2)]
    pieces += [p_ref[...]]
    total = sign_ref[0] * pieces[0].astype(F32)
    for j in range(1, 8):
        total = total + sign_ref[j] * pieces[j].astype(F32)
    mixed = (total * (1.0 / math.sqrt(inner))).astype(BF)
    z, core = place_ref[0], place_ref[1]
    for k, out_ref in enumerate((mine_ref, other_ref)):
        side = core if k == 0 else 1 - core
        for j in range(8):
            chip = jnp.bitwise_and(z + j, 7)
            spans = [
                pl.ds(pl.multiple_of(e * 2048 + (chip * 2 + side) * 128, 128), 128)
                for e in range(4)
            ]
            table = jnp.concatenate(
                [
                    jnp.concatenate([ref[:, s] for s in spans], axis=1)
                    for ref in (w0_ref, w1_ref, w2a_ref, w2b_ref, w3_ref)
                ],
                axis=0,
            )
            scale = jnp.concatenate([scale_ref[:, s] for s in spans], axis=1)
            factor = scale.astype(F32) / (LEVEL * math.sqrt(inner))
            out_ref[j] = (dot(mixed, table) * factor).astype(BF)


def expert_kernel(place_ref, *refs):
    pa, qa = refs[0:9], refs[9:18]
    pb, qb = refs[18:23], refs[23:28]
    gate_ref, up_ref, gs_ref, us_ref, gain_ref, hid_ref = refs[28:]
    z, core = place_ref[0], place_ref[1]
    width = 64 * 128
    half = pa[0].shape[1]
    gate_acc = jnp.zeros((8 * half, gate_ref.shape[1]), F32)
    up_acc = jnp.zeros((8 * half, gate_ref.shape[1]), F32)
    square = jnp.zeros((8 * half, 128), F32)

    def rows_of(a, b, j):
        if j < 4:
            parts = [a[j][i] for i in range(4)]
        elif j == 4:
            parts = [a[4][0], a[4][1], a[5][0], a[5][1]]
        else:
            parts = [a[j + 1][i] for i in range(4)]
        parts += [b[0][j], b[1][j], b[2][j] if j < 4 else b[3][j - 4], b[4][j]]
        return jnp.concatenate(parts, axis=0)

    for k in range(2):
        side = core if k == 0 else 1 - core
        a, b = (pa, pb) if k == 0 else (qa, qb)
        for j in range(8):
            chip = jnp.bitwise_and(z + j, 7)
            spans = [
                pl.ds(pl.multiple_of(e * 2048 + (chip * 2 + side) * 128, 128), 128)
                for e in range(4)
            ]
            x = rows_of(a, b, j).astype(F32)
            xx = x * x
            square = square + xx[:, 0:128] + xx[:, 128:256] + xx[:, 256:384] + xx[:, 384:512]
            gain = jnp.concatenate([gain_ref[:, s] for s in spans], axis=1)
            x = (x * gain).astype(BF)
            gate_acc = gate_acc + dot(x, jnp.concatenate([gate_ref[s, :] for s in spans], axis=0))
            up_acc = up_acc + dot(x, jnp.concatenate([up_ref[s, :] for s in spans], axis=0))
    mean = jnp.sum(square, axis=1, keepdims=True) * (1.0 / width)
    norm = lax.rsqrt(mean + 1e-05) * (1.0 / (LEVEL * math.sqrt(width)))
    gate = gate_acc * (norm * gs_ref[...].astype(F32))
    up = up_acc * (norm * us_ref[...].astype(F32))
    hid_ref[...] = (silu(gate) * up).astype(BF)


def down_kernel(place_ref, hid_ref, down_ref, scale_ref, am_ref, bm_ref, ao_ref, bo_ref):
    z, core = place_ref[0], place_ref[1]
    half = am_ref.shape[2]
    fan = 64 * down_ref.shape[0]
    hid = hid_ref[...]
    for k, (a_ref, b_ref) in enumerate(((ao_ref, bo_ref), (am_ref, bm_ref))):
        side = core if k == 1 else 1 - core
        for j in range(8):
            chip = jnp.bitwise_and(z + j, 7)
            spans = [
                pl.ds(pl.multiple_of(e * 2048 + (chip * 2 + side) * 128, 128), 128)
                for e in range(4)
            ]
            table = jnp.concatenate([down_ref[:, s] for s in spans], axis=1)
            scale = jnp.concatenate([scale_ref[:, s] for s in spans], axis=1)
            factor = scale.astype(F32) / (LEVEL * math.sqrt(fan))
            out = (dot(hid, table) * factor).astype(BF)
            for i in range(4):
                a_ref[i, j] = out[i * half : (i + 1) * half]
                b_ref[j, i] = out[(4 + i) * half : (5 + i) * half]


def add(*parts):
    total = parts[0].astype(F32)
    for part in parts[1:]:
        total = total + part.astype(F32)
    return total


def add_part(whole, part, first, axis):
    half = whole.shape[axis] // 2
    a = lax.slice_in_dim(whole, 0, half, axis=axis)
    b = lax.slice_in_dim(whole, half, 2 * half, axis=axis)
    if first:
        a = add(a, part).astype(BF)
    else:
        b = add(b, part).astype(BF)
    return jnp.concatenate([a, b], axis=axis)


def halves(a, axis):
    half = a.shape[axis] // 2
    return lax.slice_in_dim(a, 0, half, axis=axis), lax.slice_in_dim(a, half, 2 * half, axis=axis)


def scatter_ring(pieces, shift, axis):
    size = len(pieces)
    mid = size // 2
    ahead, behind = halves(pieces[mid], axis)
    for j in range(mid - 1, 0, -1):
        ahead, behind = shift(ahead, 1), shift(behind, -1)
        if j == mid - 1:
            ahead = add_part(pieces[j], ahead, True, axis)
            behind = add_part(pieces[size - j], behind, False, axis)
        else:
            ahead = add(pieces[j], ahead).astype(BF)
            behind = add(pieces[size - j], behind).astype(BF)
    return add(pieces[0], shift(ahead, 1), shift(behind, -1))


def on_device(
    mixer_input, gating_input, conv_cache, conv_weight, conv_bias, ssm_state, xproj_codes,
    xproj_scale, dtproj_codes, dtproj_scale, step_bias, decay_log, skip_gain, outproj_codes,
    outproj_scale, residual, norm_gain, expert_ids, expert_gates, gate_codes, up_codes,
    down_codes, gate_scale, up_scale, down_scale,
):
    rows, steps, slab = mixer_input.shape
    tokens = rows * steps
    group = tokens * 4
    model = outproj_codes.shape[-1]
    place = lax.axis_index("tensor")
    plane = lax.axis_index("expert")
    z, core = place // 2, place % 2
    where = jnp.stack([z, core]).astype(jnp.int32)

    own_rows = outproj_codes.reshape(128, model)
    rows_next = shift_y(own_rows, -1)
    rows_prev = shift_y(own_rows, 1)
    rows_far_a = shift_y(rows_next[:64], -1)
    rows_far_b = shift_y(rows_prev[64:], 1)

    by_plane = residual.reshape(4, rows, steps, 128).transpose(0, 2, 1, 3).reshape(4, tokens, 128)
    residual_here = jnp.zeros((tokens, 4 * 128), BF)
    for m in range(4):
        part = lax.dynamic_index_in_dim(by_plane, (plane + m) % 4, 0, keepdims=False)
        if m:
            part = shift_y(part, m)
        residual_here = lax.dynamic_update_slice(
            residual_here, part, (place * 0, ((plane + 4 - m) % 4) * 128)
        )

    act, part = call(
        conv_kernel,
        (
            jax.ShapeDtypeStruct((steps, rows, slab), F32),
            jax.ShapeDtypeStruct((tokens, xproj_codes.shape[1]), F32),
        ),
        (mixer_input, conv_cache, conv_weight, conv_bias[None], xproj_codes, xproj_scale[None]),
    )
    pair = part + swap_core(part)
    pair_bf = pair.astype(BF)
    prev, following = shift_z(pair_bf, 1), shift_z(pair_bf, -1)
    three = add(pair_bf, prev, following).astype(BF)
    two = add(pair_bf, prev).astype(BF)
    back, front = shift_z(three, 3), shift_z(two, -3)

    index = jnp.arange(slab, dtype=jnp.int32)
    column = ((plane + index // 128) % 4) * 128 + index % 128
    hadamard = sign_table(index[:, None], column[None, :], slab).astype(BF)
    rotated, new_state = call(
        scan_kernel,
        (
            jax.ShapeDtypeStruct((tokens, slab), BF),
            jax.ShapeDtypeStruct(ssm_state.shape, F32),
        ),
        (
            pair, prev, following, back, front, dtproj_codes, dtproj_scale[None], step_bias[None],
            decay_log, act, gating_input, skip_gain[None], ssm_state, hadamard,
        ),
        scratch=(pltpu.VMEM((tokens, slab), F32), pltpu.VMEM((tokens, slab), F32)),
    )

    other = swap_core(rotated)
    mine_f, other_f = rotated.astype(F32), other.astype(F32)
    paired = jnp.where(core == 0, mine_f + other_f, other_f - mine_f).astype(BF)
    prev, following = shift_z(paired, 1), shift_z(paired, -1)
    far = shift_z(jnp.concatenate([prev, paired, following]), -3)
    near = shift_z(jnp.concatenate([paired, following]), 3)
    signs = sign_table(z, (z + jnp.arange(8, dtype=jnp.int32)) % 8, 8)
    mine, others = call(
        out_kernel,
        (
            jax.ShapeDtypeStruct((8, tokens, slab), BF),
            jax.ShapeDtypeStruct((8, tokens, slab), BF),
        ),
        (
            signs, where, paired, following, prev, far, near,
            own_rows, rows_next, rows_far_a, rows_far_b, rows_prev, outproj_scale[None],
        ),
        scalars=2,
    )

    total = add(mine, swap_core(others)).astype(BF)
    ahead = shift_z(jnp.concatenate([total[4], total[3], total[2]]), 3).reshape(3, tokens, slab)
    behind = shift_z(jnp.concatenate([total[5], total[6]]), -3).reshape(2, tokens, slab)
    up_one = add(total[1], ahead[0], behind[1]).astype(BF)
    down_one = add(total[7], ahead[2]).astype(BF)
    hidden = add(
        total[0], ahead[1], behind[0], shift_z(up_one, 1), shift_z(down_one, -1), residual_here
    ).astype(BF)
    hidden_all = jnp.concatenate(
        [hidden, shift_y(hidden, -1), shift_y(hidden, 2), shift_y(hidden, 1)]
    )

    route = expert_ids.reshape(group, -1)
    gates = expert_gates.reshape(group, -1)
    capacity = 96
    half = capacity // 2
    slots = jnp.arange(capacity, dtype=jnp.int32)
    natural = jnp.arange(group, dtype=jnp.int32)
    held = natural
    held_token = (((plane + held // tokens) % 4) * rows + held % rows) * steps + (
        held % tokens
    ) // rows
    spread = (natural[:, None] == held_token[None, :]).astype(BF)
    hits = [jnp.any(route == (plane + 4 - m) % 4, axis=-1) for m in range(4)]
    members = jnp.stack(hits, axis=1).astype(jnp.int32)
    position = jnp.cumsum(members, axis=0, dtype=jnp.int32) - 1
    picks = [
        ((position[:, m][:, None] == slots[None, :]) & (members[:, m][:, None] == 1)).astype(BF)
        for m in range(4)
    ]
    select = dot(picks[0].T, spread).astype(BF)
    weight = jnp.sum(jnp.where(route == plane, gates, 0.0), axis=-1)
    slot_weight = jnp.sum(picks[0].astype(F32) * weight[:, None], axis=0)

    slot_input = dot(select, hidden_all).astype(BF)

    first, second = slot_input[:half], slot_input[half:]
    xa = jnp.stack([first, shift_x(first, -1), shift_x(first, 2), shift_x(first, 1)])
    up = [xa]
    down = [xa]
    for _ in range(3):
        up.append(shift_z(up[-1], -1))
        down.append(shift_z(down[-1], 1))
    pa = up + [shift_z(up[3][:2], -1), shift_z(down[3][2:], 1)] + down[:0:-1]
    prev, following = shift_z(second, 1), shift_z(second, -1)
    far = shift_z(jnp.stack([prev, second, following]), -3)
    near = shift_z(jnp.stack([second, following]), 3)
    xb = jnp.concatenate([second[None], following[None], far, near, prev[None]])
    b1, b3 = shift_x(xb, -1), shift_x(xb, 1)
    pb = [xb, b1, shift_x(b1[:4], -1), shift_x(b3[4:], 1), b3]
    qa = [swap_core(v) for v in pa]
    qb = [swap_core(v) for v in pb]
    expert_hidden = call(
        expert_kernel,
        jax.ShapeDtypeStruct((4 * capacity, gate_codes.shape[-1]), BF),
        (
            where, *pa, *qa, *pb, *qb, gate_codes[0], up_codes[0], gate_scale, up_scale,
            norm_gain[None],
        ),
        scalars=1,
    )
    a_shape = jax.ShapeDtypeStruct((4, 8, half, slab), BF)
    b_shape = jax.ShapeDtypeStruct((8, 4, half, slab), BF)
    a_mine, b_mine, a_other, b_other = call(
        down_kernel,
        (a_shape, b_shape, a_shape, b_shape),
        (where, expert_hidden, down_codes[0], down_scale),
        scalars=1,
    )

    a_sum = add(a_mine, swap_core(a_other)).astype(BF)
    b_sum = add(b_mine, swap_core(b_other)).astype(BF)
    a_part = scatter_ring([a_sum[i] for i in range(4)], shift_x, 0).astype(BF)
    b_part = scatter_ring([b_sum[j] for j in range(8)], shift_z, 0).astype(BF)
    a_out = scatter_ring([a_part[j] for j in range(8)], shift_z, 1)
    b_out = scatter_ring([b_part[i] for i in range(4)], shift_x, 1)
    expert_out = jnp.concatenate([a_out, b_out]) * slot_weight[:, None]
    expert_out = expert_out.astype(BF)

    moe = jnp.zeros((group, 128), F32)
    for m in range(4):
        part = lax.dynamic_slice_in_dim(expert_out, ((plane + m) % 4) * 128, 128, 1)
        if m:
            part = shift_y(part, m)
        moe = moe + dot(picks[m], part)
    hidden_here = dot(spread, lax.dynamic_slice_in_dim(hidden_all, plane * 128, 128, 1))
    layer_out = (hidden_here + moe).astype(BF).reshape(rows * 4, steps, 128)
    return layer_out, new_state


def solution(mesh):
    rows = P(("dp", "expert"), None, "tensor")
    share = P("dp", None, ("expert", "tensor"))
    units = P("expert", None, ("dp", "tensor"))
    placed = (
        rows, rows, rows, P(None, "tensor"), P("tensor"), rows, P("tensor", None), P(),
        P(None, "tensor"), P("tensor"), P("tensor"), P(None, "tensor"), P("tensor"),
        P("tensor", "expert", None, None), P(), share, P(), P("dp", None, None),
        P("dp", None, None), units, units, P("expert", ("dp", "tensor"), None),
        P("expert", ("dp", "tensor")), P("expert", ("dp", "tensor")), P("expert", None),
    )
    return jax.shard_map(
        on_device, mesh=mesh, in_specs=placed, out_specs=(share, rows), check_vma=False
    )
```

```python
import math

import jax
import jax.numpy as jnp
from jax import lax
from jax.experimental import pallas as pl
from jax.experimental.pallas import tpu as pltpu
from jax.sharding import PartitionSpec as P

BF = jnp.bfloat16
F32 = jnp.float32
LEVEL = 368.0


def sign_table(left, right, size):
    both = jnp.bitwise_and(left, right)
    parity = jnp.zeros_like(both)
    for level in range(size.bit_length() - 1):
        parity = jnp.bitwise_xor(parity, jnp.bitwise_and(jnp.right_shift(both, level), 1))
    return (1 - 2 * parity).astype(F32)


def dot(a, b):
    return jnp.dot(a, b, preferred_element_type=F32)


def dot_t(a, b):
    return lax.dot_general(a, b, (((1,), (1,)), ((), ())), preferred_element_type=F32)


def silu(x):
    return x * (1.0 / (1.0 + jnp.exp(-x)))


def shift_z(a, k):
    pairs = [(z * 2 + c, ((z + k) % 8) * 2 + c) for z in range(8) for c in range(2)]
    return lax.ppermute(a, "tensor", pairs)


def swap_core(a):
    return lax.ppermute(a, "tensor", [(t, t ^ 1) for t in range(16)])


def shift_x(a, k):
    return lax.ppermute(a, "dp", [(i, (i + k) % 4) for i in range(4)])


def shift_y(a, k):
    return lax.ppermute(a, "expert", [(i, (i + k) % 4) for i in range(4)])


def move_z(a):
    pairs = [(z * 2 + c, ((z + 1 - 2 * c) % 8) * 2 + c) for z in range(8) for c in range(2)]
    return lax.ppermute(a, "tensor", pairs)


def move_x(a, way=1):
    pairs = [
        (x * 16 + t, ((x + way * (1 - 2 * (t % 2))) % 4) * 16 + t)
        for x in range(4)
        for t in range(16)
    ]
    return lax.ppermute(a, ("dp", "tensor"), pairs)


def together(*arrays):
    return lax.optimization_barrier(arrays)


def call(kernel, outs, operands, scalars=0, scratch=(), vmem_mib=12):
    vmem = pl.BlockSpec(memory_space=pltpu.VMEM)
    smem = pl.BlockSpec(memory_space=pltpu.SMEM)
    specs = [smem] * scalars + [vmem] * (len(operands) - scalars)
    return pl.pallas_call(
        kernel,
        out_shape=outs,
        in_specs=specs,
        out_specs=jax.tree.map(lambda _: vmem, outs),
        scratch_shapes=list(scratch),
        compiler_params=pltpu.CompilerParams(vmem_limit_bytes=vmem_mib * 1024 * 1024),
    )(*operands)


def conv_kernel(mix_ref, cache_ref, taps_ref, bias_ref, table_ref, act_ref, part_ref):
    steps = mix_ref.shape[1]
    mix = mix_ref[...].astype(F32)
    cache = [cache_ref[k].astype(F32) for k in range(cache_ref.shape[0])]
    window = cache + [mix[:, k, :] for k in range(steps)]
    taps = taps_ref[...].astype(F32)
    acts = []
    for t in range(steps):
        total = bias_ref[...]
        for k in range(taps.shape[0]):
            total = total + taps[k : k + 1, :] * window[t + k]
        act = silu(total)
        act_ref[t] = act
        acts.append(act)
    flat = jnp.concatenate(acts, axis=0).astype(BF)
    part_ref[...] = dot_t(flat, table_ref[...])


def scan_kernel(
    q_ref, p_ref, m_ref, a_ref, b_ref, sum_scale_ref, table_ref, scale_ref, bias_ref, decay_ref, act_ref,
    gate_ref, skip_ref, state_ref, had_ref, rot_ref, new_ref, delta_ref, read_ref,
):
    rank = table_ref.shape[0]
    nstate = decay_ref.shape[0]
    rows, steps = gate_ref.shape[0], gate_ref.shape[1]
    proj = q_ref[...] + p_ref[...].astype(F32) + m_ref[...].astype(F32)
    proj = proj + a_ref[...].astype(F32) + b_ref[...].astype(F32)
    inner = 16 * state_ref.shape[2]
    proj = proj * (sum_scale_ref[...].astype(F32) / (LEVEL * math.sqrt(inner)))
    factor = scale_ref[...].astype(F32) / (LEVEL * math.sqrt(rank))
    pre = dot(proj[:, :rank].astype(BF), table_ref[...]) * factor + bias_ref[...]
    delta_ref[...] = jnp.maximum(pre, 0.0) + jnp.log1p(jnp.exp(-jnp.abs(pre)))
    coef = jnp.transpose(proj[:, rank:])
    decay = -jnp.exp(decay_ref[...])
    for r in range(rows):
        state = state_ref[r]
        for t in range(steps):
            row = t * rows + r
            delta = delta_ref[row : row + 1, :]
            current = act_ref[t, r : r + 1, :]
            into = coef[0:nstate, row : row + 1]
            out = coef[nstate : 2 * nstate, row : row + 1]
            state = jnp.exp(delta * decay) * state + (delta * current) * into
            read_ref[row : row + 1, :] = jnp.sum(out * state, axis=0, keepdims=True)
        new_ref[r] = state
    gate = gate_ref[...].astype(F32)
    gated = []
    for t in range(steps):
        readout = read_ref[t * rows : (t + 1) * rows, :] + skip_ref[...] * act_ref[t]
        gated.append(readout * silu(gate[:, t, :]))
    gated = jnp.concatenate(gated, axis=0).astype(BF)
    rot_ref[...] = dot(gated, had_ref[...]).astype(BF)


def chip_ahead(place_ref, r):
    return jnp.bitwise_and((1 - 2 * place_ref[1]) * r, 7)


def column_spans(place_ref, up, u):
    z, core = place_ref[0], place_ref[1]
    chip = jnp.bitwise_and(z + up, 7)
    side = core if u == 0 else 1 - core
    return [
        pl.ds(pl.multiple_of(e * 2048 + (chip * 2 + side) * 128, 128), 128) for e in range(4)
    ]


def out_kernel(
    sign_ref, place_ref, own_ref, m_ref, p_ref, far_ref, back_ref, table_ref, scale_ref,
    mine_ref, other_ref, stay_ref,
):
    rows = own_ref.shape[0]
    inner = 64 * own_ref.shape[1]
    pieces = [own_ref[...], m_ref[...]]
    pieces += [far_ref[i * rows : (i + 1) * rows] for i in range(3)]
    pieces += [back_ref[i * rows : (i + 1) * rows] for i in range(2)]
    pieces += [p_ref[...]]
    total = sign_ref[0] * pieces[0].astype(F32)
    for j in range(1, 8):
        total = total + sign_ref[j] * pieces[j].astype(F32)
    mixed = (total * (1.0 / math.sqrt(inner))).astype(BF)
    for r in range(8):
        j = chip_ahead(place_ref, r)
        for u in range(2):
            spans = column_spans(place_ref, j, u)
            table = jnp.concatenate([table_ref[:, s] for s in spans], axis=1)
            scale = jnp.concatenate([scale_ref[:, s] for s in spans], axis=1)
            factor = scale.astype(F32) / (LEVEL * math.sqrt(inner))
            out = (dot(mixed, table) * factor).astype(BF)
            back, other = (8 - r) % 8, 1 - u
            if r == 0:
                stay_ref[u] = out
            if 1 <= r < 4:
                mine_ref[(r - 1) * 2 + u] = out
            if r == 4 and u == 0:
                mine_ref[6] = out
            if r == 4 and u == 1:
                other_ref[6] = out
            if r > 4:
                other_ref[(back - 1) * 2 + other] = out


def route_kernel(
    place_ref, stay_ref, come_ref, back_ref, residual_ref, spread_ref, pick_ref, out_ref, sum_ref
):
    plane = place_ref[2]
    total = add(stay_ref[0], come_ref[...], back_ref[...]).astype(BF)
    sum_ref[...] = dot(spread_ref[...], total)
    own = pl.ds(pl.multiple_of(plane * 128, 128), 128)
    sum_ref[:, own] = sum_ref[:, own] + residual_ref[...].astype(F32)
    values = sum_ref[...].astype(BF)
    sum_ref[...] = values.astype(F32)
    tokens = values.shape[0] // 4
    slots = pick_ref.shape[1]
    for m in range(4):
        out_ref[m, :slots] = dot(pick_ref[m], values).astype(BF)
        to = pl.ds(pl.multiple_of(jnp.bitwise_and(plane + m, 3) * 128, 128), 128)
        share = sum_ref[:, to]
        share = [share[i * tokens : (i + 1) * tokens] for i in range(4)]
        out_ref[m, slots:] = jnp.concatenate(share, axis=1).astype(BF)


def expert_kernel(place_ref, *refs):
    a = refs[0:8]
    a4 = refs[8]
    p = refs[9:15]
    p4 = refs[15]
    xb, b1, b2, q1, q2 = refs[16:18], refs[18:20], refs[20], refs[21:23], refs[23]
    gate_ref, up_ref, gs_ref, us_ref, gain_ref, hid_ref = refs[24:]
    width = 64 * 128
    height = 4 * (a4.shape[1] + b2.shape[1])
    units = gate_ref.shape[0]
    acc = jnp.zeros((height, 2 * units), F32)
    square = jnp.zeros((height, 128), F32)
    for r in range(8):
        for u in range(2):
            if r < 4:
                parts = [a[2 * r + u][m] for m in range(4)]
            elif r == 4 and u == 0:
                parts = [a4[m] for m in range(4)]
            elif r == 4:
                parts = [p4[(4 - m) % 4] for m in range(4)]
            else:
                parts = [p[2 * (7 - r) + 1 - u][(4 - m) % 4] for m in range(4)]
            j = chip_ahead(place_ref, 8 - r)
            parts += [xb[u][j], b1[u][j], b2[j] if u == 0 else q2[j], q1[1 - u][j]]
            spans = column_spans(place_ref, j, u)
            x = jnp.concatenate(parts, axis=0).astype(F32)
            xx = x * x
            square = square + xx[:, 0:128] + xx[:, 128:256] + xx[:, 256:384] + xx[:, 384:512]
            gain = jnp.concatenate([gain_ref[:, s] for s in spans], axis=1)
            x = (x * gain).astype(BF)
            table = [jnp.concatenate([ref[:, s] for s in spans], axis=1) for ref in (gate_ref, up_ref)]
            acc = acc + dot_t(x, jnp.concatenate(table, axis=0))
    mean = jnp.sum(square, axis=1, keepdims=True) * (1.0 / width)
    norm = lax.rsqrt(mean + 1e-05) * (1.0 / (LEVEL * math.sqrt(width)))
    gate = acc[:, :units] * (norm * gs_ref[...].astype(F32))
    up = acc[:, units:] * (norm * us_ref[...].astype(F32))
    hid_ref[...] = (silu(gate) * up).astype(BF)


def down_kernel(
    place_ref, hid_ref, down_ref, scale_ref,
    a_mine, a_other, a_stay, b_mine, b_other, b_stay,
):
    half = a_stay.shape[2]
    fan = 64 * down_ref.shape[0]
    hid = hid_ref[...]
    for r in range(8):
        j = chip_ahead(place_ref, r)
        for u in range(2):
            spans = column_spans(place_ref, j, u)
            table = jnp.concatenate([down_ref[:, s] for s in spans], axis=1)
            scale = jnp.concatenate([scale_ref[:, s] for s in spans], axis=1)
            factor = scale.astype(F32) / (LEVEL * math.sqrt(fan))
            out = (dot(hid, table) * factor).astype(BF)
            a = [out[m * half : (m + 1) * half] for m in range(4)]
            b = [out[(4 + m) * half : (5 + m) * half] for m in range(4)]
            back, other = (8 - r) % 8, 1 - u
            a_stay[u, j] = a[0]
            a_mine[u, j] = a[3]
            a_other[other, j] = a[1]
            if u == 0:
                a_mine[2, j] = a[2]
            else:
                a_other[2, j] = a[2]
            for k in range(4):
                if r == 0:
                    b_stay[u, k] = b[(4 - k) % 4]
                if 1 <= r < 4:
                    b_mine[(r - 1) * 2 + u, k] = b[(4 - k) % 4]
                if r == 4 and u == 0:
                    b_mine[6, k] = b[(4 - k) % 4]
                if r == 4 and u == 1:
                    b_other[6, k] = b[k]
                if r > 4:
                    b_other[(back - 1) * 2 + other, k] = b[k]


def add(*parts):
    total = parts[0].astype(F32)
    for part in parts[1:]:
        total = total + part.astype(F32)
    return total


def sum_bf(*parts):
    return add(*parts).astype(BF)


def scatter_z(mine, other):
    got = swap_core(other)
    one = move_z(sum_bf(mine[6], got[6]))
    two = move_z(sum_bf(mine[5], got[5]))
    one, two = together(one, two)
    one = move_z(sum_bf(mine[4], got[4], one))
    two = move_z(sum_bf(mine[3], got[3], two))
    one, two = together(one, two)
    one = move_z(sum_bf(mine[2], got[2], one))
    two = move_z(sum_bf(mine[1], got[1], two))
    one, two = together(one, two)
    one = move_z(sum_bf(mine[0], got[0], one))
    return one, two


def on_device(
    mixer_input, gating_input, conv_cache, conv_weight, conv_bias, ssm_state, xproj_codes,
    xproj_scale, dtproj_codes, dtproj_scale, step_bias, decay_log, skip_gain, outproj_codes,
    outproj_scale, residual, norm_gain, expert_ids, expert_gates, gate_codes, up_codes,
    down_codes, gate_scale, up_scale, down_scale,
):
    rows, steps, slab = mixer_input.shape
    tokens = rows * steps
    group = tokens * 4
    model = outproj_codes.shape[-1]
    place = lax.axis_index("tensor")
    plane = lax.axis_index("expert")
    z, core = place // 2, place % 2
    where = jnp.stack([z, core, plane]).astype(jnp.int32)

    route = expert_ids.reshape(group, -1)
    gates = expert_gates.reshape(group, -1)
    capacity = 96
    half = capacity // 2
    slots = jnp.arange(capacity, dtype=jnp.int32)
    natural = jnp.arange(group, dtype=jnp.int32)
    held = natural
    held_token = (((plane + 4 - held // tokens) % 4) * rows + held % rows) * steps + (
        held % tokens
    ) // rows
    spread = (natural[:, None] == held_token[None, :]).astype(BF)
    hits = [jnp.any(route == (plane + m) % 4, axis=-1) for m in range(4)]
    members = jnp.stack(hits, axis=1).astype(jnp.int32)
    position = jnp.cumsum(members, axis=0, dtype=jnp.int32) - 1
    picks = jnp.stack(
        [
            (position[:, m][None, :] == slots[:, None]) & (members[:, m][None, :] == 1)
            for m in range(4)
        ]
    ).astype(BF)
    weight = jnp.sum(jnp.where(route == plane, gates, 0.0), axis=-1)
    slot_weight = jnp.sum(picks[0].astype(F32) * weight[None, :], axis=1)

    act, part = call(
        conv_kernel,
        (
            jax.ShapeDtypeStruct((steps, rows, slab), F32),
            jax.ShapeDtypeStruct((tokens, xproj_codes.shape[1]), F32),
        ),
        (
            mixer_input, conv_cache.transpose(1, 0, 2), conv_weight, conv_bias[None],
            xproj_codes.T,
        ),
        vmem_mib=56,
    )
    pair = part + swap_core(part)
    pair_bf = pair.astype(BF)
    prev, following = shift_z(pair_bf, 1), shift_z(pair_bf, -1)
    three = add(pair_bf, prev, following).astype(BF)
    two = add(pair_bf, prev).astype(BF)
    back, front = shift_z(three, 3), shift_z(two, -3)

    index = jnp.arange(slab, dtype=jnp.int32)
    column = ((plane + index // 128) % 4) * 128 + index % 128
    hadamard = sign_table(index[:, None], column[None, :], slab).astype(BF)
    rotated, new_state = call(
        scan_kernel,
        (
            jax.ShapeDtypeStruct((tokens, slab), BF),
            jax.ShapeDtypeStruct(ssm_state.shape, F32),
        ),
        (
            pair, prev, following, back, front, xproj_scale[None], dtproj_codes, dtproj_scale[None], step_bias[None],
            decay_log, act, gating_input, skip_gain[None], ssm_state, hadamard,
        ),
        scratch=(pltpu.VMEM((tokens, slab), F32), pltpu.VMEM((tokens, slab), F32)),
    )

    rotated = jnp.concatenate(
        [rotated[:, :128]] + [shift_y(rotated[:, m * 128 : (m + 1) * 128], m) for m in (1, 2, 3)]
    )
    other = swap_core(rotated)
    mine_f, other_f = rotated.astype(F32), other.astype(F32)
    paired = jnp.where(core == 0, mine_f + other_f, other_f - mine_f).astype(BF)
    prev, following = shift_z(paired, 1), shift_z(paired, -1)
    far = shift_z(jnp.concatenate([prev, paired, following]), -3)
    near = shift_z(jnp.concatenate([paired, following]), 3)
    signs = sign_table(z, (z + jnp.arange(8, dtype=jnp.int32)) % 8, 8)
    mine, others, stay = call(
        out_kernel,
        (
            jax.ShapeDtypeStruct((7, group, slab), BF),
            jax.ShapeDtypeStruct((7, group, slab), BF),
            jax.ShapeDtypeStruct((2, group, slab), BF),
        ),
        (
            signs, where, paired, following, prev, far, near, outproj_codes.reshape(128, model),
            outproj_scale[None],
        ),
        scalars=2,
    )

    one, two = scatter_z(mine, others)
    back = swap_core(sum_bf(stay[1], two))
    shares = call(
        route_kernel,
        jax.ShapeDtypeStruct((4, capacity + tokens, slab), BF),
        (where, stay, one, back, residual.reshape(group, 128), spread, picks),
        scalars=1,
        scratch=(pltpu.VMEM((group, slab), F32),),
    )
    hidden = sum_bf(shares[0], *[shift_y(shares[m], m) for m in (1, 2, 3)])
    slot_input = hidden[:capacity]
    hidden_here = jnp.concatenate([hidden[capacity:, i * 128 : (i + 1) * 128] for i in range(4)])

    first, second = slot_input[:half], slot_input[half:]
    up_x, down_x, far_x = shift_x(first, -1), shift_x(first, 1), shift_x(first, 2)
    prev, following = shift_z(second, 1), shift_z(second, -1)
    behind_x = jnp.where(core == 0, down_x, up_x)
    before_x = jnp.where(core == 0, up_x, down_x)
    mine = jnp.stack([first, behind_x, far_x, before_x])
    mine, prev, following = together(mine, prev, following)
    back = swap_core(mine)
    xa = [mine, jnp.stack([back[0], back[3], back[2], back[1]])]
    far = shift_z(jnp.stack([prev, second, following]), -3)
    near = shift_z(jnp.stack([second, following]), 3)
    a1 = [move_z(v) for v in xa]
    far, near, *a1 = together(far, near, *a1)
    mine = jnp.concatenate([second[None], following[None], far, near, prev[None]])
    xb = [mine, swap_core(mine)]
    a2 = [move_z(v) for v in a1]
    b1 = [move_x(v) for v in xb]
    p1 = [swap_core(v) for v in a1]
    a3 = [move_z(v) for v in a2]
    b2 = move_x(b1[0])
    p2 = [swap_core(v) for v in a2]
    q1 = [swap_core(v) for v in b1]
    a4 = move_z(a3[0])
    p3 = [swap_core(v) for v in a3]
    q2 = swap_core(b2)
    p4 = swap_core(a4)
    expert_hidden = call(
        expert_kernel,
        jax.ShapeDtypeStruct((4 * capacity, gate_codes.shape[-1]), BF),
        (
            where, *xa, *a1, *a2, *a3, a4, *p1, *p2, *p3, p4, *xb, *b1, b2, *q1, q2,
            gate_codes[0].T, up_codes[0].T, gate_scale, up_scale, norm_gain[None],
        ),
        scalars=1,
        vmem_mib=24,
    )
    a_three = jax.ShapeDtypeStruct((3, 8, half, slab), BF)
    a_both = jax.ShapeDtypeStruct((2, 8, half, slab), BF)
    b_shape = jax.ShapeDtypeStruct((7, 4, half, slab), BF)
    a_mine, a_other, a_stay, b_mine, b_other, b_stay = call(
        down_kernel,
        (
            a_three, a_three, a_both,
            b_shape, b_shape, jax.ShapeDtypeStruct((2, 4, half, slab), BF),
        ),
        (where, expert_hidden, down_codes[0], down_scale),
        scalars=1,
        vmem_mib=20,
    )

    a_got = swap_core(a_other)
    b_got = swap_core(b_other)
    v = move_x(sum_bf(a_mine[2], a_got[2]))
    one = move_z(sum_bf(b_mine[6], b_got[6]))
    u = move_x(sum_bf(a_mine[1], a_got[1]))
    two = move_z(sum_bf(b_mine[5], b_got[5]))
    v = move_x(sum_bf(a_mine[0], a_got[0], v))
    one = move_z(sum_bf(b_mine[4], b_got[4], one))
    two = move_z(sum_bf(b_mine[3], b_got[3], two))
    back = swap_core(sum_bf(a_stay[1], u))
    one = move_z(sum_bf(b_mine[2], b_got[2], one))
    a_tot = sum_bf(a_stay[0], v, back)
    two = move_z(sum_bf(b_mine[1], b_got[1], two))
    ahead = shift_z(jnp.stack([a_tot[4], a_tot[3], a_tot[2]]), 3)
    behind = shift_z(jnp.stack([a_tot[5], a_tot[6]]), -3)
    one = move_z(sum_bf(b_mine[0], b_got[0], one))
    up_one = shift_z(sum_bf(a_tot[1], ahead[0], behind[1]), 1)
    down_one = shift_z(sum_bf(a_tot[7], ahead[2]), -1)
    back = sum_bf(b_stay[1], two)
    back = swap_core(jnp.stack([back[0], back[3], back[2], back[1]]))
    b_tot = sum_bf(b_stay[0], one, back)
    a_out = add(a_tot[0], ahead[1], behind[0], up_one, down_one)
    b_out = add(b_tot[0], move_x(b_tot[1]), move_x(b_tot[3], -1), shift_x(b_tot[2], 2))
    expert_out = jnp.concatenate([a_out, b_out]) * slot_weight[:, None]
    expert_out = expert_out.astype(BF)

    moe = hidden_here.astype(F32)
    for m in range(4):
        part = lax.dynamic_slice_in_dim(expert_out, ((plane + 4 - m) % 4) * 128, 128, 1)
        if m:
            part = shift_y(part, 4 - m)
        moe = moe + dot(picks[m].T, part)
    return moe.astype(BF).reshape(rows * 4, steps, 128), new_state


def solution(mesh):
    rows = P(("dp", "expert"), None, "tensor")
    share = P("dp", None, ("expert", "tensor"))
    units = P("expert", None, ("dp", "tensor"))
    placed = (
        rows, rows, rows, P(None, "tensor"), P("tensor"), rows, P("tensor", None), P(),
        P(None, "tensor"), P("tensor"), P("tensor"), P(None, "tensor"), P("tensor"),
        P("tensor", "expert", None, None), P(), share, P(), P("dp", None, None),
        P("dp", None, None), units, units, P("expert", ("dp", "tensor"), None),
        P("expert", ("dp", "tensor")), P("expert", ("dp", "tensor")), P("expert", None),
    )
    return jax.shard_map(
        on_device, mesh=mesh, in_specs=placed, out_specs=(share, rows), check_vma=False
    )
```

```python
import math

import jax
import jax.numpy as jnp
from jax import lax
from jax.experimental import pallas as pl
from jax.experimental.pallas import tpu as pltpu
from jax.sharding import PartitionSpec as P

BF = jnp.bfloat16
F32 = jnp.float32
LEVEL = 368.0


def sign_table(left, right, size):
    both = jnp.bitwise_and(left, right)
    parity = jnp.zeros_like(both)
    for level in range(size.bit_length() - 1):
        parity = jnp.bitwise_xor(parity, jnp.bitwise_and(jnp.right_shift(both, level), 1))
    return (1 - 2 * parity).astype(F32)


def dot(a, b):
    return jnp.dot(a, b, preferred_element_type=F32)


def dot_t(a, b):
    return lax.dot_general(a, b, (((1,), (1,)), ((), ())), preferred_element_type=F32)


def silu(x):
    return x * (1.0 / (1.0 + jnp.exp(-x)))


def shift_z(a, k):
    pairs = [(z * 2 + c, ((z + k) % 8) * 2 + c) for z in range(8) for c in range(2)]
    return lax.ppermute(a, "tensor", pairs)


def swap_core(a):
    return lax.ppermute(a, "tensor", [(t, t ^ 1) for t in range(16)])


def shift_x(a, k):
    return lax.ppermute(a, "dp", [(i, (i + k) % 4) for i in range(4)])


def shift_y(a, k):
    return lax.ppermute(a, "expert", [(i, (i + k) % 4) for i in range(4)])


def move_z(a):
    pairs = [(z * 2 + c, ((z + 1 - 2 * c) % 8) * 2 + c) for z in range(8) for c in range(2)]
    return lax.ppermute(a, "tensor", pairs)


def move_x(a, way=1):
    pairs = [
        (x * 16 + t, ((x + way * (1 - 2 * (t % 2))) % 4) * 16 + t)
        for x in range(4)
        for t in range(16)
    ]
    return lax.ppermute(a, ("dp", "tensor"), pairs)


def together(*arrays):
    return lax.optimization_barrier(arrays)


def call(kernel, outs, operands, scalars=0, scratch=(), vmem_mib=12, flops=0):
    vmem = pl.BlockSpec(memory_space=pltpu.VMEM)
    smem = pl.BlockSpec(memory_space=pltpu.SMEM)
    moved = sum(v.size * v.dtype.itemsize for v in (*operands, *jax.tree.leaves(outs)))
    specs = [smem] * scalars + [vmem] * (len(operands) - scalars)
    return pl.pallas_call(
        kernel,
        out_shape=outs,
        in_specs=specs,
        out_specs=jax.tree.map(lambda _: vmem, outs),
        scratch_shapes=list(scratch),
        compiler_params=pltpu.CompilerParams(vmem_limit_bytes=vmem_mib * 1024 * 1024),
        cost_estimate=pl.CostEstimate(flops=flops, bytes_accessed=moved, transcendentals=0),
    )(*operands)


def conv_kernel(mix_ref, cache_ref, taps_ref, bias_ref, table_ref, act_ref, part_ref):
    steps = mix_ref.shape[1]
    mix = mix_ref[...].astype(F32)
    cache = [cache_ref[k].astype(F32) for k in range(cache_ref.shape[0])]
    window = cache + [mix[:, k, :] for k in range(steps)]
    taps = taps_ref[...].astype(F32)
    acts = []
    for t in range(steps):
        total = bias_ref[...]
        for k in range(taps.shape[0]):
            total = total + taps[k : k + 1, :] * window[t + k]
        act = silu(total)
        act_ref[t] = act
        acts.append(act)
    flat = jnp.concatenate(acts, axis=0).astype(BF)
    part_ref[...] = dot_t(flat, table_ref[...])


def scan_kernel(
    q_ref, p_ref, m_ref, a_ref, b_ref, sum_scale_ref, table_ref, scale_ref, bias_ref, decay_ref, act_ref,
    gate_ref, skip_ref, state_ref, had_ref, rot_ref, new_ref, delta_ref, read_ref,
):
    rank = table_ref.shape[0]
    nstate = decay_ref.shape[0]
    rows, steps = gate_ref.shape[0], gate_ref.shape[1]
    proj = q_ref[...] + p_ref[...].astype(F32) + m_ref[...].astype(F32)
    proj = proj + a_ref[...].astype(F32) + b_ref[...].astype(F32)
    inner = 16 * state_ref.shape[2]
    proj = proj * (sum_scale_ref[...].astype(F32) / (LEVEL * math.sqrt(inner)))
    factor = scale_ref[...].astype(F32) / (LEVEL * math.sqrt(rank))
    pre = dot(proj[:, :rank].astype(BF), table_ref[...]) * factor + bias_ref[...]
    delta_ref[...] = jnp.maximum(pre, 0.0) + jnp.log1p(jnp.exp(-jnp.abs(pre)))
    coef = jnp.transpose(proj[:, rank:])
    decay = -jnp.exp(decay_ref[...])
    for r in range(rows):
        state = state_ref[r]
        for t in range(steps):
            row = t * rows + r
            delta = delta_ref[row : row + 1, :]
            current = act_ref[t, r : r + 1, :]
            into = coef[0:nstate, row : row + 1]
            out = coef[nstate : 2 * nstate, row : row + 1]
            state = jnp.exp(delta * decay) * state + (delta * current) * into
            read_ref[row : row + 1, :] = jnp.sum(out * state, axis=0, keepdims=True)
        new_ref[r] = state
    gate = gate_ref[...].astype(F32)
    gated = []
    for t in range(steps):
        readout = read_ref[t * rows : (t + 1) * rows, :] + skip_ref[...] * act_ref[t]
        gated.append(readout * silu(gate[:, t, :]))
    gated = jnp.concatenate(gated, axis=0).astype(BF)
    rot_ref[...] = dot(gated, had_ref[...]).astype(BF)


def chip_ahead(place_ref, r):
    return jnp.bitwise_and((1 - 2 * place_ref[1]) * r, 7)


def column_spans(place_ref, up, u):
    z, core = place_ref[0], place_ref[1]
    chip = jnp.bitwise_and(z + up, 7)
    side = core if u == 0 else 1 - core
    return [
        pl.ds(pl.multiple_of(e * 2048 + (chip * 2 + side) * 128, 128), 128) for e in range(4)
    ]


def out_kernel(
    sign_ref, place_ref, own_ref, m_ref, p_ref, far_ref, back_ref, table_ref, scale_ref,
    mine_ref, other_ref, stay_ref,
):
    rows = own_ref.shape[0]
    inner = 64 * own_ref.shape[1]
    pieces = [own_ref[...], m_ref[...]]
    pieces += [far_ref[i * rows : (i + 1) * rows] for i in range(3)]
    pieces += [back_ref[i * rows : (i + 1) * rows] for i in range(2)]
    pieces += [p_ref[...]]
    total = sign_ref[0] * pieces[0].astype(F32)
    for j in range(1, 8):
        total = total + sign_ref[j] * pieces[j].astype(F32)
    mixed = (total * (1.0 / math.sqrt(inner))).astype(BF)
    for r in range(8):
        j = chip_ahead(place_ref, r)
        for u in range(2):
            spans = column_spans(place_ref, j, u)
            table = jnp.concatenate([table_ref[:, s] for s in spans], axis=1)
            scale = jnp.concatenate([scale_ref[:, s] for s in spans], axis=1)
            factor = scale.astype(F32) / (LEVEL * math.sqrt(inner))
            out = (dot(mixed, table) * factor).astype(BF)
            back, other = (8 - r) % 8, 1 - u
            if r == 0:
                stay_ref[u] = out
            if 1 <= r < 4:
                mine_ref[(r - 1) * 2 + u] = out
            if r == 4 and u == 0:
                mine_ref[6] = out
            if r == 4 and u == 1:
                other_ref[6] = out
            if r > 4:
                other_ref[(back - 1) * 2 + other] = out


def route_kernel(
    place_ref, stay_ref, come_ref, back_ref, residual_ref, spread_ref, pick_ref, out_ref, sum_ref
):
    plane = place_ref[2]
    total = add(stay_ref[0], come_ref[...], back_ref[...]).astype(BF)
    sum_ref[...] = dot(spread_ref[...], total)
    own = pl.ds(pl.multiple_of(plane * 128, 128), 128)
    sum_ref[:, own] = sum_ref[:, own] + residual_ref[...].astype(F32)
    values = sum_ref[...].astype(BF)
    sum_ref[...] = values.astype(F32)
    tokens = values.shape[0] // 4
    slots = pick_ref.shape[1]
    for m in range(4):
        out_ref[m, :slots] = dot(pick_ref[m], values).astype(BF)
        to = pl.ds(pl.multiple_of(jnp.bitwise_and(plane + m, 3) * 128, 128), 128)
        share = sum_ref[:, to]
        share = [share[i * tokens : (i + 1) * tokens] for i in range(4)]
        out_ref[m, slots:] = jnp.concatenate(share, axis=1).astype(BF)


def expert_kernel(place_ref, *refs):
    a, a4, p, p4 = refs[0:4], refs[4], refs[5:8], refs[8]
    gate_ref, up_ref, gs_ref, us_ref, gain_ref, hid_ref = refs[9:]
    height = 4 * a4.shape[1]
    width = 64 * 128
    units = gate_ref.shape[0]
    acc = jnp.zeros((height, 2 * units), F32)
    square = jnp.zeros((height, 128), F32)
    for r in range(8):
        for u in range(2):
            if r < 4:
                parts = [a[r][u, m] for m in range(4)]
            elif r == 4 and u == 0:
                parts = [a4[m] for m in range(4)]
            elif r == 4:
                parts = [p4[(4 - m) % 4] for m in range(4)]
            else:
                parts = [p[7 - r][1 - u, (4 - m) % 4] for m in range(4)]
            spans = column_spans(place_ref, chip_ahead(place_ref, 8 - r), u)
            x = jnp.concatenate(parts, axis=0).astype(F32)
            xx = x * x
            square = square + xx[:, 0:128] + xx[:, 128:256] + xx[:, 256:384] + xx[:, 384:512]
            gain = jnp.concatenate([gain_ref[:, s] for s in spans], axis=1)
            x = (x * gain).astype(BF)
            table = [jnp.concatenate([ref[:, s] for s in spans], axis=1) for ref in (gate_ref, up_ref)]
            acc = acc + dot_t(x, jnp.concatenate(table, axis=0))
    mean = jnp.sum(square, axis=1, keepdims=True) * (1.0 / width)
    norm = lax.rsqrt(mean + 1e-05) * (1.0 / (LEVEL * math.sqrt(width)))
    gate = acc[:, :units] * (norm * gs_ref[...].astype(F32))
    up = acc[:, units:] * (norm * us_ref[...].astype(F32))
    hid_ref[...] = (silu(gate) * up).astype(BF)


def down_kernel(place_ref, hid_ref, down_ref, scale_ref, mine, other, stay):
    half = hid_ref.shape[0] // 4
    fan = 64 * down_ref.shape[0]
    hid = hid_ref[...]
    for r in range(8):
        for u in range(2):
            spans = column_spans(place_ref, chip_ahead(place_ref, r), u)
            table = jnp.concatenate([down_ref[:, s] for s in spans], axis=1)
            scale = jnp.concatenate([scale_ref[:, s] for s in spans], axis=1)
            factor = scale.astype(F32) / (LEVEL * math.sqrt(fan))
            out = (dot(hid, table) * factor).astype(BF)
            rows = [out[m * half : (m + 1) * half] for m in range(4)]
            back = (8 - r) % 8
            for k in range(4):
                if r == 0:
                    stay[u, k] = rows[(4 - k) % 4]
                if 1 <= r < 4:
                    mine[(r - 1) * 2 + u, k] = rows[(4 - k) % 4]
                if r == 4 and u == 0:
                    mine[6, k] = rows[(4 - k) % 4]
                if r == 4 and u == 1:
                    other[6, k] = rows[k]
                if r > 4:
                    other[(back - 1) * 2 + 1 - u, k] = rows[k]


def near_kernel(mine_ref, got_ref, come_ref, sum_ref):
    come = [come_ref[...], None] if len(come_ref.shape) == 3 else [come_ref[0], come_ref[1]]
    for u in range(2):
        total = add(mine_ref[u], got_ref[u])
        if come[u] is not None:
            total = total + come[u].astype(F32)
        sum_ref[u] = total.astype(BF)


def near_sum(mine, got, come, start):
    shape = (2,) + mine.shape[1:]
    zeros = (0,) * (len(shape) - 1)
    pair = pl.BlockSpec(shape, lambda i: (start // 2,) + zeros)
    return pl.pallas_call(
        near_kernel,
        out_shape=jax.ShapeDtypeStruct(shape, BF),
        grid=(1,),
        in_specs=[pair, pair, pl.BlockSpec(come.shape, lambda i: (0,) * come.ndim)],
        out_specs=pl.BlockSpec(shape, lambda i: (0,) + zeros),
        compiler_params=pltpu.CompilerParams(vmem_limit_bytes=8 * 1024 * 1024),
        cost_estimate=pl.CostEstimate(flops=0, bytes_accessed=0, transcendentals=0),
    )(mine, got, come)


def add(*parts):
    total = parts[0].astype(F32)
    for part in parts[1:]:
        total = total + part.astype(F32)
    return total


def sum_bf(*parts):
    return add(*parts).astype(BF)


def scatter_z(mine, other):
    got = swap_core(other)
    one = move_z(sum_bf(mine[6], got[6]))
    two = move_z(sum_bf(mine[5], got[5]))
    one, two = together(one, two)
    one = move_z(sum_bf(mine[4], got[4], one))
    two = move_z(sum_bf(mine[3], got[3], two))
    one, two = together(one, two)
    one = move_z(sum_bf(mine[2], got[2], one))
    two = move_z(sum_bf(mine[1], got[1], two))
    one, two = together(one, two)
    one = move_z(sum_bf(mine[0], got[0], one))
    return one, two


def on_device(
    mixer_input, gating_input, conv_cache, conv_weight, conv_bias, ssm_state, xproj_codes,
    xproj_scale, dtproj_codes, dtproj_scale, step_bias, decay_log, skip_gain, outproj_codes,
    outproj_scale, residual, norm_gain, expert_ids, expert_gates, gate_codes, up_codes,
    down_codes, gate_scale, up_scale, down_scale,
):
    rows, steps, slab = mixer_input.shape
    tokens = rows * steps
    group = tokens * 4
    model = outproj_codes.shape[-1]
    place = lax.axis_index("tensor")
    plane = lax.axis_index("expert")
    z, core = place // 2, place % 2
    where = jnp.stack([z, core, plane]).astype(jnp.int32)

    route = expert_ids.reshape(group, -1)
    gates = expert_gates.reshape(group, -1)
    capacity = 96
    half = capacity // 2
    slots = jnp.arange(capacity, dtype=jnp.int32)
    natural = jnp.arange(group, dtype=jnp.int32)
    held = natural
    held_token = (((plane + 4 - held // tokens) % 4) * rows + held % rows) * steps + (
        held % tokens
    ) // rows
    spread = (natural[:, None] == held_token[None, :]).astype(BF)
    hits = [jnp.any(route == (plane + m) % 4, axis=-1) for m in range(4)]
    members = jnp.stack(hits, axis=1).astype(jnp.int32)
    position = jnp.cumsum(members, axis=0, dtype=jnp.int32) - 1
    picks = jnp.stack(
        [
            (position[:, m][None, :] == slots[:, None]) & (members[:, m][None, :] == 1)
            for m in range(4)
        ]
    ).astype(BF)
    weight = jnp.sum(jnp.where(route == plane, gates, 0.0), axis=-1)
    slot_weight = jnp.sum(picks[0].astype(F32) * weight[None, :], axis=1)

    act, part = call(
        conv_kernel,
        (
            jax.ShapeDtypeStruct((steps, rows, slab), F32),
            jax.ShapeDtypeStruct((tokens, xproj_codes.shape[1]), F32),
        ),
        (
            mixer_input, conv_cache.transpose(1, 0, 2), conv_weight, conv_bias[None],
            xproj_codes.T,
        ),
        vmem_mib=56,
    )
    pair = part + swap_core(part)
    pair_bf = pair.astype(BF)
    prev, following = shift_z(pair_bf, 1), shift_z(pair_bf, -1)
    three = add(pair_bf, prev, following).astype(BF)
    two = add(pair_bf, prev).astype(BF)
    back, front = shift_z(three, 3), shift_z(two, -3)

    index = jnp.arange(slab, dtype=jnp.int32)
    column = ((plane + index // 128) % 4) * 128 + index % 128
    hadamard = sign_table(index[:, None], column[None, :], slab).astype(BF)
    rotated, new_state = call(
        scan_kernel,
        (
            jax.ShapeDtypeStruct((tokens, slab), BF),
            jax.ShapeDtypeStruct(ssm_state.shape, F32),
        ),
        (
            pair, prev, following, back, front, xproj_scale[None], dtproj_codes, dtproj_scale[None], step_bias[None],
            decay_log, act, gating_input, skip_gain[None], ssm_state, hadamard,
        ),
        scratch=(pltpu.VMEM((tokens, slab), F32), pltpu.VMEM((tokens, slab), F32)),
    )

    rotated = jnp.concatenate(
        [rotated[:, :128]] + [shift_y(rotated[:, m * 128 : (m + 1) * 128], m) for m in (1, 2, 3)]
    )
    other = swap_core(rotated)
    mine_f, other_f = rotated.astype(F32), other.astype(F32)
    paired = jnp.where(core == 0, mine_f + other_f, other_f - mine_f).astype(BF)
    prev, following = shift_z(paired, 1), shift_z(paired, -1)
    far = shift_z(jnp.concatenate([prev, paired, following]), -3)
    near = shift_z(jnp.concatenate([paired, following]), 3)
    signs = sign_table(z, (z + jnp.arange(8, dtype=jnp.int32)) % 8, 8)
    mine, others, stay = call(
        out_kernel,
        (
            jax.ShapeDtypeStruct((7, group, slab), BF),
            jax.ShapeDtypeStruct((7, group, slab), BF),
            jax.ShapeDtypeStruct((2, group, slab), BF),
        ),
        (
            signs, where, paired, following, prev, far, near, outproj_codes.reshape(128, model),
            outproj_scale[None],
        ),
        scalars=2,
    )

    one, two = scatter_z(mine, others)
    back = swap_core(sum_bf(stay[1], two))
    shares = call(
        route_kernel,
        jax.ShapeDtypeStruct((4, capacity + tokens, slab), BF),
        (where, stay, one, back, residual.reshape(group, 128), spread, picks),
        scalars=1,
        scratch=(pltpu.VMEM((group, slab), F32),),
    )
    hidden = sum_bf(shares[0], *[shift_y(shares[m], m) for m in (1, 2, 3)])
    slot_input = hidden[:capacity]
    hidden_here = jnp.concatenate([hidden[capacity:, i * 128 : (i + 1) * 128] for i in range(4)])

    up_x, down_x, far_x = (
        shift_x(slot_input, -1), shift_x(slot_input, 1), shift_x(slot_input, 2)
    )
    behind_x = jnp.where(core == 0, down_x, up_x)
    before_x = jnp.where(core == 0, up_x, down_x)
    mine = jnp.stack([slot_input, behind_x, far_x, before_x])
    back = swap_core(mine)
    tables = (gate_codes[0].T, up_codes[0].T, gate_scale, up_scale, norm_gain[None])
    carried = []
    for h in range(2):
        part, other = mine[:, h * half : (h + 1) * half], back[:, h * half : (h + 1) * half]
        carried.append([jnp.stack([part, jnp.stack([other[0], other[3], other[2], other[1]])])])
    starts = together(*[move_z(chain[-1]) for chain in carried])
    for chain, v in zip(carried, starts):
        chain.append(v)
    for _ in range(2):
        for chain in carried:
            chain.append(move_z(chain[-1]))
    for chain in carried:
        chain.append(move_z(chain[-1][0]))
    outs, gots, sums = [], [], []
    for chain in carried:
        backs = [swap_core(v) for v in chain[1:]]
        height, units = 2 * capacity, gate_codes.shape[-1]
        hid = call(
            expert_kernel,
            jax.ShapeDtypeStruct((height, units), BF),
            (where, *chain, *backs, *tables),
            scalars=1,
            vmem_mib=16,
            flops=4 * height * units * model,
        )
        seven = jax.ShapeDtypeStruct((7, 4, half, slab), BF)
        mine, other, stay = call(
            down_kernel,
            (seven, seven, jax.ShapeDtypeStruct((2, 4, half, slab), BF)),
            (where, hid, down_codes[0], down_scale),
            scalars=1,
            flops=2 * height * units * model,
        )
        got = swap_core(other)
        outs.append((mine, stay))
        gots.append(got)
        sums.append(move_z(sum_bf(mine[6], got[6])))

    for start in (4, 2, 0):
        sums = [
            move_z(near_sum(out[0], got, v, start)) for out, got, v in zip(outs, gots, sums)
        ]
    ends = []
    for (_, stay), v in zip(outs, sums):
        back = sum_bf(stay[1], v[1])
        back = swap_core(jnp.stack([back[0], back[3], back[2], back[1]]))
        total = sum_bf(stay[0], v[0], back)
        ends.append(
            add(total[0], move_x(total[1]), move_x(total[3], -1), shift_x(total[2], 2))
        )
    a_out, b_out = ends
    expert_out = jnp.concatenate([a_out, b_out]) * slot_weight[:, None]
    expert_out = expert_out.astype(BF)

    moe = hidden_here.astype(F32)
    for m in range(4):
        part = lax.dynamic_slice_in_dim(expert_out, ((plane + 4 - m) % 4) * 128, 128, 1)
        if m:
            part = shift_y(part, 4 - m)
        moe = moe + dot(picks[m].T, part)
    return moe.astype(BF).reshape(rows * 4, steps, 128), new_state


def solution(mesh):
    rows = P(("dp", "expert"), None, "tensor")
    share = P("dp", None, ("expert", "tensor"))
    units = P("expert", None, ("dp", "tensor"))
    placed = (
        rows, rows, rows, P(None, "tensor"), P("tensor"), rows, P("tensor", None), P(),
        P(None, "tensor"), P("tensor"), P("tensor"), P(None, "tensor"), P("tensor"),
        P("tensor", "expert", None, None), P(), share, P(), P("dp", None, None),
        P("dp", None, None), units, units, P("expert", ("dp", "tensor"), None),
        P("expert", ("dp", "tensor")), P("expert", ("dp", "tensor")), P("expert", None),
    )
    return jax.shard_map(
        on_device, mesh=mesh, in_specs=placed, out_specs=(share, rows), check_vma=False
    )
```

```python
import math

import jax
import jax.numpy as jnp
from jax import lax
from jax.experimental import pallas as pl
from jax.experimental.pallas import tpu as pltpu
from jax.sharding import PartitionSpec as P

BF = jnp.bfloat16
F32 = jnp.float32
LEVEL = 368.0


def sign_table(left, right, size):
    both = jnp.bitwise_and(left, right)
    parity = jnp.zeros_like(both)
    for level in range(size.bit_length() - 1):
        parity = jnp.bitwise_xor(parity, jnp.bitwise_and(jnp.right_shift(both, level), 1))
    return (1 - 2 * parity).astype(F32)


def dot(a, b):
    return jnp.dot(a, b, preferred_element_type=F32)


def dot_t(a, b):
    return lax.dot_general(a, b, (((1,), (1,)), ((), ())), preferred_element_type=F32)


def silu(x):
    return x * (1.0 / (1.0 + jnp.exp(-x)))


def shift_z(a, k):
    pairs = [(z * 2 + c, ((z + k) % 8) * 2 + c) for z in range(8) for c in range(2)]
    return lax.ppermute(a, "tensor", pairs)


def swap_core(a):
    return lax.ppermute(a, "tensor", [(t, t ^ 1) for t in range(16)])


def shift_x(a, k):
    return lax.ppermute(a, "dp", [(i, (i + k) % 4) for i in range(4)])


def shift_y(a, k):
    return lax.ppermute(a, "expert", [(i, (i + k) % 4) for i in range(4)])


def move_z(a):
    pairs = [(z * 2 + c, ((z + 1 - 2 * c) % 8) * 2 + c) for z in range(8) for c in range(2)]
    return lax.ppermute(a, "tensor", pairs)


def move_x(a, way=1):
    pairs = [
        (x * 16 + t, ((x + way * (1 - 2 * (t % 2))) % 4) * 16 + t)
        for x in range(4)
        for t in range(16)
    ]
    return lax.ppermute(a, ("dp", "tensor"), pairs)


def together(*arrays):
    return lax.optimization_barrier(arrays)


def call(kernel, outs, operands, scalars=0, scratch=(), vmem_mib=12, flops=0):
    vmem = pl.BlockSpec(memory_space=pltpu.VMEM)
    smem = pl.BlockSpec(memory_space=pltpu.SMEM)
    moved = sum(v.size * v.dtype.itemsize for v in (*operands, *jax.tree.leaves(outs)))
    specs = [smem] * scalars + [vmem] * (len(operands) - scalars)
    return pl.pallas_call(
        kernel,
        out_shape=outs,
        in_specs=specs,
        out_specs=jax.tree.map(lambda _: vmem, outs),
        scratch_shapes=list(scratch),
        compiler_params=pltpu.CompilerParams(vmem_limit_bytes=vmem_mib * 1024 * 1024),
        cost_estimate=pl.CostEstimate(flops=flops, bytes_accessed=moved, transcendentals=0),
    )(*operands)


def conv_kernel(mix_ref, cache_ref, taps_ref, bias_ref, table_ref, act_ref, part_ref):
    steps = mix_ref.shape[1]
    mix = mix_ref[...].astype(F32)
    cache = [cache_ref[k].astype(F32) for k in range(cache_ref.shape[0])]
    window = cache + [mix[:, k, :] for k in range(steps)]
    taps = taps_ref[...].astype(F32)
    acts = []
    for t in range(steps):
        total = bias_ref[...]
        for k in range(taps.shape[0]):
            total = total + taps[k : k + 1, :] * window[t + k]
        act = silu(total)
        act_ref[t] = act
        acts.append(act)
    flat = jnp.concatenate(acts, axis=0).astype(BF)
    part_ref[...] = dot_t(flat, table_ref[...])


def scan_kernel(
    q_ref, p_ref, m_ref, a_ref, b_ref, sum_scale_ref, table_ref, scale_ref, bias_ref, decay_ref, act_ref,
    gate_ref, skip_ref, state_ref, had_ref, rot_ref, new_ref, delta_ref, read_ref,
):
    rank = table_ref.shape[0]
    nstate = decay_ref.shape[0]
    rows, steps = gate_ref.shape[0], gate_ref.shape[1]
    proj = q_ref[...] + p_ref[...].astype(F32) + m_ref[...].astype(F32)
    proj = proj + a_ref[...].astype(F32) + b_ref[...].astype(F32)
    inner = 16 * state_ref.shape[2]
    proj = proj * (sum_scale_ref[...].astype(F32) / (LEVEL * math.sqrt(inner)))
    factor = scale_ref[...].astype(F32) / (LEVEL * math.sqrt(rank))
    pre = dot(proj[:, :rank].astype(BF), table_ref[...]) * factor + bias_ref[...]
    delta_ref[...] = jnp.maximum(pre, 0.0) + jnp.log1p(jnp.exp(-jnp.abs(pre)))
    coef = jnp.transpose(proj[:, rank:])
    decay = -jnp.exp(decay_ref[...])
    for r in range(rows):
        state = state_ref[r]
        for t in range(steps):
            row = t * rows + r
            delta = delta_ref[row : row + 1, :]
            current = act_ref[t, r : r + 1, :]
            into = coef[0:nstate, row : row + 1]
            out = coef[nstate : 2 * nstate, row : row + 1]
            state = jnp.exp(delta * decay) * state + (delta * current) * into
            read_ref[row : row + 1, :] = jnp.sum(out * state, axis=0, keepdims=True)
        new_ref[r] = state
    gate = gate_ref[...].astype(F32)
    gated = []
    for t in range(steps):
        readout = read_ref[t * rows : (t + 1) * rows, :] + skip_ref[...] * act_ref[t]
        gated.append(readout * silu(gate[:, t, :]))
    gated = jnp.concatenate(gated, axis=0).astype(BF)
    rot_ref[...] = dot(gated, had_ref[...]).astype(BF)


def chip_ahead(place_ref, r):
    return jnp.bitwise_and((1 - 2 * place_ref[1]) * r, 7)


def column_spans(place_ref, up, u):
    z, core = place_ref[0], place_ref[1]
    chip = jnp.bitwise_and(z + up, 7)
    side = core if u == 0 else 1 - core
    return [
        pl.ds(pl.multiple_of(e * 2048 + (chip * 2 + side) * 128, 128), 128) for e in range(4)
    ]


def out_kernel(
    sign_ref, place_ref, own_ref, m_ref, p_ref, far_ref, back_ref, table_ref, scale_ref,
    mine_ref, other_ref, stay_ref,
):
    rows = own_ref.shape[0]
    inner = 64 * own_ref.shape[1]
    pieces = [own_ref[...], m_ref[...]]
    pieces += [far_ref[i * rows : (i + 1) * rows] for i in range(3)]
    pieces += [back_ref[i * rows : (i + 1) * rows] for i in range(2)]
    pieces += [p_ref[...]]
    total = sign_ref[0] * pieces[0].astype(F32)
    for j in range(1, 8):
        total = total + sign_ref[j] * pieces[j].astype(F32)
    mixed = (total * (1.0 / math.sqrt(inner))).astype(BF)
    for r in range(8):
        j = chip_ahead(place_ref, r)
        for u in range(2):
            spans = column_spans(place_ref, j, u)
            table = jnp.concatenate([table_ref[:, s] for s in spans], axis=1)
            scale = jnp.concatenate([scale_ref[:, s] for s in spans], axis=1)
            factor = scale.astype(F32) / (LEVEL * math.sqrt(inner))
            out = (dot(mixed, table) * factor).astype(BF)
            back, other = (8 - r) % 8, 1 - u
            if r == 0:
                stay_ref[u] = out
            if 1 <= r < 4:
                mine_ref[(r - 1) * 2 + u] = out
            if r == 4 and u == 0:
                mine_ref[6] = out
            if r == 4 and u == 1:
                other_ref[6] = out
            if r > 4:
                other_ref[(back - 1) * 2 + other] = out


def route_kernel(
    place_ref, stay_ref, come_ref, back_ref, residual_ref, spread_ref, pick_ref, out_ref, sum_ref
):
    plane = place_ref[2]
    total = add(stay_ref[0], come_ref[...], back_ref[...]).astype(BF)
    sum_ref[...] = dot(spread_ref[...], total)
    own = pl.ds(pl.multiple_of(plane * 128, 128), 128)
    sum_ref[:, own] = sum_ref[:, own] + residual_ref[...].astype(F32)
    values = sum_ref[...].astype(BF)
    sum_ref[...] = values.astype(F32)
    tokens = values.shape[0] // 4
    slots = pick_ref.shape[1]
    for m in range(4):
        out_ref[m, :slots] = dot(pick_ref[m], values).astype(BF)
        to = pl.ds(pl.multiple_of(jnp.bitwise_and(plane + m, 3) * 128, 128), 128)
        share = sum_ref[:, to]
        share = [share[i * tokens : (i + 1) * tokens] for i in range(4)]
        out_ref[m, slots:] = jnp.concatenate(share, axis=1).astype(BF)


def expert_kernel(place_ref, *refs):
    chains = [refs[0:9], refs[9:18]]
    gate_ref, up_ref, gs_ref, us_ref, gain_ref, hid_ref = refs[18:]
    height = hid_ref.shape[0]
    width = 64 * 128
    units = gate_ref.shape[0]
    acc = jnp.zeros((height, 2 * units), F32)
    square = jnp.zeros((height, 128), F32)
    for r in range(8):
        for u in range(2):
            parts = []
            for chain in chains:
                a, a4, p, p4 = chain[0:4], chain[4], chain[5:8], chain[8]
                for m in range(4):
                    if r < 4:
                        parts.append(a[r][u, m])
                    elif r == 4:
                        parts.append(a4[m] if u == 0 else p4[(4 - m) % 4])
                    else:
                        parts.append(p[7 - r][1 - u, (4 - m) % 4])
            spans = column_spans(place_ref, chip_ahead(place_ref, 8 - r), u)
            x = jnp.concatenate(parts, axis=0).astype(F32)
            xx = x * x
            square = square + xx[:, 0:128] + xx[:, 128:256] + xx[:, 256:384] + xx[:, 384:512]
            gain = jnp.concatenate([gain_ref[:, s] for s in spans], axis=1)
            x = (x * gain).astype(BF)
            table = [jnp.concatenate([ref[:, s] for s in spans], axis=1) for ref in (gate_ref, up_ref)]
            acc = acc + dot_t(x, jnp.concatenate(table, axis=0))
    mean = jnp.sum(square, axis=1, keepdims=True) * (1.0 / width)
    norm = lax.rsqrt(mean + 1e-05) * (1.0 / (LEVEL * math.sqrt(width)))
    gate = acc[:, :units] * (norm * gs_ref[...].astype(F32))
    up = acc[:, units:] * (norm * us_ref[...].astype(F32))
    hid_ref[...] = (silu(gate) * up).astype(BF)


def down_kernel(place_ref, hid_ref, down_ref, scale_ref, *outs):
    half = hid_ref.shape[0] // 8
    fan = 64 * down_ref.shape[0]
    hid = hid_ref[...]
    for r in range(8):
        for u in range(2):
            spans = column_spans(place_ref, chip_ahead(place_ref, r), u)
            table = jnp.concatenate([down_ref[:, s] for s in spans], axis=1)
            scale = jnp.concatenate([scale_ref[:, s] for s in spans], axis=1)
            factor = scale.astype(F32) / (LEVEL * math.sqrt(fan))
            out = (dot(hid, table) * factor).astype(BF)
            back = (8 - r) % 8
            for h in range(2):
                mine, other, stay = outs[3 * h : 3 * h + 3]
                rows = [out[(4 * h + m) * half : (4 * h + m + 1) * half] for m in range(4)]
                for k in range(4):
                    if r == 0:
                        stay[u, k] = rows[(4 - k) % 4]
                    if 1 <= r < 4:
                        mine[(r - 1) * 2 + u, k] = rows[(4 - k) % 4]
                    if r == 4 and u == 0:
                        mine[6, k] = rows[(4 - k) % 4]
                    if r == 4 and u == 1:
                        other[6, k] = rows[k]
                    if r > 4:
                        other[(back - 1) * 2 + 1 - u, k] = rows[k]


def near_kernel(mine_ref, got_ref, come_ref, sum_ref):
    come = [come_ref[...], None] if len(come_ref.shape) == 3 else [come_ref[0], come_ref[1]]
    for u in range(2):
        total = add(mine_ref[u], got_ref[u])
        if come[u] is not None:
            total = total + come[u].astype(F32)
        sum_ref[u] = total.astype(BF)


def near_sum(mine, got, come, start):
    shape = (2,) + mine.shape[1:]
    zeros = (0,) * (len(shape) - 1)
    pair = pl.BlockSpec(shape, lambda i: (start // 2,) + zeros)
    return pl.pallas_call(
        near_kernel,
        out_shape=jax.ShapeDtypeStruct(shape, BF),
        grid=(1,),
        in_specs=[pair, pair, pl.BlockSpec(come.shape, lambda i: (0,) * come.ndim)],
        out_specs=pl.BlockSpec(shape, lambda i: (0,) + zeros),
        compiler_params=pltpu.CompilerParams(vmem_limit_bytes=8 * 1024 * 1024),
        cost_estimate=pl.CostEstimate(flops=0, bytes_accessed=0, transcendentals=0),
    )(mine, got, come)


def add(*parts):
    total = parts[0].astype(F32)
    for part in parts[1:]:
        total = total + part.astype(F32)
    return total


def sum_bf(*parts):
    return add(*parts).astype(BF)


def scatter_z(mine, other):
    got = swap_core(other)
    one = move_z(sum_bf(mine[6], got[6]))
    two = move_z(sum_bf(mine[5], got[5]))
    one, two = together(one, two)
    one = move_z(sum_bf(mine[4], got[4], one))
    two = move_z(sum_bf(mine[3], got[3], two))
    one, two = together(one, two)
    one = move_z(sum_bf(mine[2], got[2], one))
    two = move_z(sum_bf(mine[1], got[1], two))
    one, two = together(one, two)
    one = move_z(sum_bf(mine[0], got[0], one))
    return one, two


def on_device(
    mixer_input, gating_input, conv_cache, conv_weight, conv_bias, ssm_state, xproj_codes,
    xproj_scale, dtproj_codes, dtproj_scale, step_bias, decay_log, skip_gain, outproj_codes,
    outproj_scale, residual, norm_gain, expert_ids, expert_gates, gate_codes, up_codes,
    down_codes, gate_scale, up_scale, down_scale,
):
    rows, steps, slab = mixer_input.shape
    tokens = rows * steps
    group = tokens * 4
    model = outproj_codes.shape[-1]
    place = lax.axis_index("tensor")
    plane = lax.axis_index("expert")
    z, core = place // 2, place % 2
    where = jnp.stack([z, core, plane]).astype(jnp.int32)

    route = expert_ids.reshape(group, -1)
    gates = expert_gates.reshape(group, -1)
    capacity = 96
    half = capacity // 2
    slots = jnp.arange(capacity, dtype=jnp.int32)
    natural = jnp.arange(group, dtype=jnp.int32)
    held = natural
    held_token = (((plane + 4 - held // tokens) % 4) * rows + held % rows) * steps + (
        held % tokens
    ) // rows
    spread = (natural[:, None] == held_token[None, :]).astype(BF)
    hits = [jnp.any(route == (plane + m) % 4, axis=-1) for m in range(4)]
    members = jnp.stack(hits, axis=1).astype(jnp.int32)
    position = jnp.cumsum(members, axis=0, dtype=jnp.int32) - 1
    picks = jnp.stack(
        [
            (position[:, m][None, :] == slots[:, None]) & (members[:, m][None, :] == 1)
            for m in range(4)
        ]
    ).astype(BF)
    weight = jnp.sum(jnp.where(route == plane, gates, 0.0), axis=-1)
    slot_weight = jnp.sum(picks[0].astype(F32) * weight[None, :], axis=1)

    act, part = call(
        conv_kernel,
        (
            jax.ShapeDtypeStruct((steps, rows, slab), F32),
            jax.ShapeDtypeStruct((tokens, xproj_codes.shape[1]), F32),
        ),
        (
            mixer_input, conv_cache.transpose(1, 0, 2), conv_weight, conv_bias[None],
            xproj_codes.T,
        ),
        vmem_mib=48,
    )
    pair = part + swap_core(part)
    pair_bf = pair.astype(BF)
    prev, following = shift_z(pair_bf, 1), shift_z(pair_bf, -1)
    three = add(pair_bf, prev, following).astype(BF)
    two = add(pair_bf, prev).astype(BF)
    back, front = shift_z(three, 3), shift_z(two, -3)

    index = jnp.arange(slab, dtype=jnp.int32)
    column = ((plane + index // 128) % 4) * 128 + index % 128
    hadamard = sign_table(index[:, None], column[None, :], slab).astype(BF)
    rotated, new_state = call(
        scan_kernel,
        (
            jax.ShapeDtypeStruct((tokens, slab), BF),
            jax.ShapeDtypeStruct(ssm_state.shape, F32),
        ),
        (
            pair, prev, following, back, front, xproj_scale[None], dtproj_codes, dtproj_scale[None], step_bias[None],
            decay_log, act, gating_input, skip_gain[None], ssm_state, hadamard,
        ),
        scratch=(pltpu.VMEM((tokens, slab), F32), pltpu.VMEM((tokens, slab), F32)),
    )

    rotated = jnp.concatenate(
        [rotated[:, :128]] + [shift_y(rotated[:, m * 128 : (m + 1) * 128], m) for m in (1, 2, 3)]
    )
    other = swap_core(rotated)
    mine_f, other_f = rotated.astype(F32), other.astype(F32)
    paired = jnp.where(core == 0, mine_f + other_f, other_f - mine_f).astype(BF)
    prev, following = shift_z(paired, 1), shift_z(paired, -1)
    far = shift_z(jnp.concatenate([prev, paired, following]), -3)
    near = shift_z(jnp.concatenate([paired, following]), 3)
    signs = sign_table(z, (z + jnp.arange(8, dtype=jnp.int32)) % 8, 8)
    mine, others, stay = call(
        out_kernel,
        (
            jax.ShapeDtypeStruct((7, group, slab), BF),
            jax.ShapeDtypeStruct((7, group, slab), BF),
            jax.ShapeDtypeStruct((2, group, slab), BF),
        ),
        (
            signs, where, paired, following, prev, far, near, outproj_codes.reshape(128, model),
            outproj_scale[None],
        ),
        scalars=2,
    )

    one, two = scatter_z(mine, others)
    back = swap_core(sum_bf(stay[1], two))
    shares = call(
        route_kernel,
        jax.ShapeDtypeStruct((4, capacity + tokens, slab), BF),
        (where, stay, one, back, residual.reshape(group, 128), spread, picks),
        scalars=1,
        scratch=(pltpu.VMEM((group, slab), F32),),
    )
    hidden = sum_bf(shares[0], *[shift_y(shares[m], m) for m in (1, 2, 3)])
    slot_input = hidden[:capacity]
    hidden_here = jnp.concatenate([hidden[capacity:, i * 128 : (i + 1) * 128] for i in range(4)])

    up_x, down_x, far_x = (
        shift_x(slot_input, -1), shift_x(slot_input, 1), shift_x(slot_input, 2)
    )
    behind_x = jnp.where(core == 0, down_x, up_x)
    before_x = jnp.where(core == 0, up_x, down_x)
    mine = jnp.stack([slot_input, behind_x, far_x, before_x])
    back = swap_core(mine)
    tables = (gate_codes[0].T, up_codes[0].T, gate_scale, up_scale, norm_gain[None])
    carried = []
    for h in range(2):
        part, other = mine[:, h * half : (h + 1) * half], back[:, h * half : (h + 1) * half]
        carried.append([jnp.stack([part, jnp.stack([other[0], other[3], other[2], other[1]])])])
    starts = together(*[move_z(chain[-1]) for chain in carried])
    for chain, v in zip(carried, starts):
        chain.append(v)
    for _ in range(2):
        for chain in carried:
            chain.append(move_z(chain[-1]))
    for chain in carried:
        chain.append(move_z(chain[-1][0]))
    chains = [v for chain in carried for v in (*chain, *[swap_core(w) for w in chain[1:]])]
    height, units = 4 * capacity, gate_codes.shape[-1]
    hid = call(
        expert_kernel,
        jax.ShapeDtypeStruct((height, units), BF),
        (where, *chains, *tables),
        scalars=1,
        vmem_mib=24,
        flops=4 * height * units * model,
    )
    seven = jax.ShapeDtypeStruct((7, 4, half, slab), BF)
    two = jax.ShapeDtypeStruct((2, 4, half, slab), BF)
    down = call(
        down_kernel,
        (seven, seven, two, seven, seven, two),
        (where, hid, down_codes[0], down_scale),
        scalars=1,
        vmem_mib=20,
        flops=2 * height * units * model,
    )
    outs, gots, sums = [], [], []
    for mine, other, stay in (down[:3], down[3:]):
        got = swap_core(other)
        outs.append((mine, stay))
        gots.append(got)
        sums.append(move_z(sum_bf(mine[6], got[6])))
    sums = together(*sums)

    for start in (4, 2, 0):
        sums = [
            move_z(near_sum(out[0], got, v, start)) for out, got, v in zip(outs, gots, sums)
        ]
    ends = []
    for (_, stay), v in zip(outs, sums):
        back = sum_bf(stay[1], v[1])
        back = swap_core(jnp.stack([back[0], back[3], back[2], back[1]]))
        ends.append(sum_bf(stay[0], v[0], back))
    total = jnp.concatenate(ends, axis=1)
    expert_out = add(
        total[0], move_x(total[1]), move_x(total[3], -1), shift_x(total[2], 2)
    )
    expert_out = expert_out * slot_weight[:, None]
    expert_out = expert_out.astype(BF)

    moe = hidden_here.astype(F32)
    for m in range(4):
        part = lax.dynamic_slice_in_dim(expert_out, ((plane + 4 - m) % 4) * 128, 128, 1)
        if m:
            part = shift_y(part, 4 - m)
        moe = moe + dot(picks[m].T, part)
    return moe.astype(BF).reshape(rows * 4, steps, 128), new_state


def solution(mesh):
    rows = P(("dp", "expert"), None, "tensor")
    share = P("dp", None, ("expert", "tensor"))
    units = P("expert", None, ("dp", "tensor"))
    placed = (
        rows, rows, rows, P(None, "tensor"), P("tensor"), rows, P("tensor", None), P(),
        P(None, "tensor"), P("tensor"), P("tensor"), P(None, "tensor"), P("tensor"),
        P("tensor", "expert", None, None), P(), share, P(), P("dp", None, None),
        P("dp", None, None), units, units, P("expert", ("dp", "tensor"), None),
        P("expert", ("dp", "tensor")), P("expert", ("dp", "tensor")), P("expert", None),
    )
    return jax.shard_map(
        on_device, mesh=mesh, in_specs=placed, out_specs=(share, rows), check_vma=False
    )
```

```python
import math

import jax
import jax.numpy as jnp
from jax import lax
from jax.experimental import pallas as pl
from jax.experimental.pallas import tpu as pltpu
from jax.sharding import PartitionSpec as P

BF = jnp.bfloat16
F32 = jnp.float32
LEVEL = 368.0


def sign_table(left, right, size):
    both = jnp.bitwise_and(left, right)
    parity = jnp.zeros_like(both)
    for level in range(size.bit_length() - 1):
        parity = jnp.bitwise_xor(parity, jnp.bitwise_and(jnp.right_shift(both, level), 1))
    return (1 - 2 * parity).astype(F32)


def dot(a, b):
    return jnp.dot(a, b, preferred_element_type=F32)


def dot_t(a, b):
    return lax.dot_general(a, b, (((1,), (1,)), ((), ())), preferred_element_type=F32)


def silu(x):
    return x * (1.0 / (1.0 + jnp.exp(-x)))


def shift_z(a, k):
    pairs = [(z * 2 + c, ((z + k) % 8) * 2 + c) for z in range(8) for c in range(2)]
    return lax.ppermute(a, "tensor", pairs)


def swap_core(a):
    return lax.ppermute(a, "tensor", [(t, t ^ 1) for t in range(16)])


def shift_x(a, k):
    return lax.ppermute(a, "dp", [(i, (i + k) % 4) for i in range(4)])


def shift_y(a, k):
    return lax.ppermute(a, "expert", [(i, (i + k) % 4) for i in range(4)])


def move_z(a):
    pairs = [(z * 2 + c, ((z + 1 - 2 * c) % 8) * 2 + c) for z in range(8) for c in range(2)]
    return lax.ppermute(a, "tensor", pairs)


def move_x(a, way=1):
    pairs = [
        (x * 16 + t, ((x + way * (1 - 2 * (t % 2))) % 4) * 16 + t)
        for x in range(4)
        for t in range(16)
    ]
    return lax.ppermute(a, ("dp", "tensor"), pairs)


def together(*arrays):
    return lax.optimization_barrier(arrays)


def call(kernel, outs, operands, scalars=0, scratch=(), vmem_mib=12, flops=0):
    vmem = pl.BlockSpec(memory_space=pltpu.VMEM)
    smem = pl.BlockSpec(memory_space=pltpu.SMEM)
    moved = sum(v.size * v.dtype.itemsize for v in (*operands, *jax.tree.leaves(outs)))
    specs = [smem] * scalars + [vmem] * (len(operands) - scalars)
    return pl.pallas_call(
        kernel,
        out_shape=outs,
        in_specs=specs,
        out_specs=jax.tree.map(lambda _: vmem, outs),
        scratch_shapes=list(scratch),
        compiler_params=pltpu.CompilerParams(vmem_limit_bytes=vmem_mib * 1024 * 1024),
        cost_estimate=pl.CostEstimate(flops=flops, bytes_accessed=moved, transcendentals=0),
    )(*operands)


def conv_kernel(mix_ref, cache_ref, taps_ref, bias_ref, table_ref, act_ref, part_ref):
    steps = mix_ref.shape[1]
    mix = mix_ref[...].astype(F32)
    cache = [cache_ref[k].astype(F32) for k in range(cache_ref.shape[0])]
    window = cache + [mix[:, k, :] for k in range(steps)]
    taps = taps_ref[...].astype(F32)
    acts = []
    for t in range(steps):
        total = bias_ref[...]
        for k in range(taps.shape[0]):
            total = total + taps[k : k + 1, :] * window[t + k]
        act = silu(total)
        act_ref[t] = act
        acts.append(act)
    flat = jnp.concatenate(acts, axis=0).astype(BF)
    part_ref[...] = dot_t(flat, table_ref[...])


def scan_kernel(
    q_ref, p_ref, m_ref, a_ref, b_ref, sum_scale_ref, table_ref, scale_ref, bias_ref, decay_ref, act_ref,
    gate_ref, skip_ref, state_ref, had_ref, rot_ref, new_ref, delta_ref, read_ref,
):
    rank = table_ref.shape[0]
    nstate = decay_ref.shape[0]
    rows, steps = gate_ref.shape[0], gate_ref.shape[1]
    proj = q_ref[...] + p_ref[...].astype(F32) + m_ref[...].astype(F32)
    proj = proj + a_ref[...].astype(F32) + b_ref[...].astype(F32)
    inner = 16 * state_ref.shape[2]
    proj = proj * (sum_scale_ref[...].astype(F32) / (LEVEL * math.sqrt(inner)))
    factor = scale_ref[...].astype(F32) / (LEVEL * math.sqrt(rank))
    pre = dot(proj[:, :rank].astype(BF), table_ref[...]) * factor + bias_ref[...]
    delta_ref[...] = jnp.maximum(pre, 0.0) + jnp.log1p(jnp.exp(-jnp.abs(pre)))
    coef = jnp.transpose(proj[:, rank:])
    decay = -jnp.exp(decay_ref[...])
    for r in range(rows):
        state = state_ref[r]
        for t in range(steps):
            row = t * rows + r
            delta = delta_ref[row : row + 1, :]
            current = act_ref[t, r : r + 1, :]
            into = coef[0:nstate, row : row + 1]
            out = coef[nstate : 2 * nstate, row : row + 1]
            state = jnp.exp(delta * decay) * state + (delta * current) * into
            read_ref[row : row + 1, :] = jnp.sum(out * state, axis=0, keepdims=True)
        new_ref[r] = state
    gate = gate_ref[...].astype(F32)
    gated = []
    for t in range(steps):
        readout = read_ref[t * rows : (t + 1) * rows, :] + skip_ref[...] * act_ref[t]
        gated.append(readout * silu(gate[:, t, :]))
    gated = jnp.concatenate(gated, axis=0).astype(BF)
    rot_ref[...] = dot(gated, had_ref[...]).astype(BF)


def chip_ahead(place_ref, r):
    return jnp.bitwise_and((1 - 2 * place_ref[1]) * r, 7)


def column_spans(place_ref, up, u):
    z, core = place_ref[0], place_ref[1]
    chip = jnp.bitwise_and(z + up, 7)
    side = core if u == 0 else 1 - core
    return [
        pl.ds(pl.multiple_of(e * 2048 + (chip * 2 + side) * 128, 128), 128) for e in range(4)
    ]


def out_kernel(
    sign_ref, place_ref, own_ref, m_ref, p_ref, far_ref, back_ref, table_ref, scale_ref,
    mine_ref, other_ref, stay_ref,
):
    rows = own_ref.shape[0]
    inner = 64 * own_ref.shape[1]
    pieces = [own_ref[...], m_ref[...]]
    pieces += [far_ref[i * rows : (i + 1) * rows] for i in range(3)]
    pieces += [back_ref[i * rows : (i + 1) * rows] for i in range(2)]
    pieces += [p_ref[...]]
    total = sign_ref[0] * pieces[0].astype(F32)
    for j in range(1, 8):
        total = total + sign_ref[j] * pieces[j].astype(F32)
    mixed = (total * (1.0 / math.sqrt(inner))).astype(BF)
    for r in range(8):
        j = chip_ahead(place_ref, r)
        for u in range(2):
            spans = column_spans(place_ref, j, u)
            table = jnp.concatenate([table_ref[:, s] for s in spans], axis=1)
            scale = jnp.concatenate([scale_ref[:, s] for s in spans], axis=1)
            factor = scale.astype(F32) / (LEVEL * math.sqrt(inner))
            out = (dot(mixed, table) * factor).astype(BF)
            back, other = (8 - r) % 8, 1 - u
            if r == 0:
                stay_ref[u] = out
            if 1 <= r < 4:
                mine_ref[(r - 1) * 2 + u] = out
            if r == 4 and u == 0:
                mine_ref[6] = out
            if r == 4 and u == 1:
                other_ref[6] = out
            if r > 4:
                other_ref[(back - 1) * 2 + other] = out


def route_kernel(
    place_ref, stay_ref, come_ref, back_ref, residual_ref, spread_ref, pick_ref, out_ref, sum_ref
):
    plane = place_ref[2]
    total = add(stay_ref[0], come_ref[...], back_ref[...]).astype(BF)
    sum_ref[...] = dot(spread_ref[...], total)
    own = pl.ds(pl.multiple_of(plane * 128, 128), 128)
    sum_ref[:, own] = sum_ref[:, own] + residual_ref[...].astype(F32)
    values = sum_ref[...].astype(BF)
    sum_ref[...] = values.astype(F32)
    tokens = values.shape[0] // 4
    slots = pick_ref.shape[1]
    for m in range(4):
        out_ref[m, :slots] = dot(pick_ref[m], values).astype(BF)
        to = pl.ds(pl.multiple_of(jnp.bitwise_and(plane + m, 3) * 128, 128), 128)
        share = sum_ref[:, to]
        share = [share[i * tokens : (i + 1) * tokens] for i in range(4)]
        out_ref[m, slots:] = jnp.concatenate(share, axis=1).astype(BF)


def expert_kernel(place_ref, *refs):
    chains = [refs[0:9], refs[9:18]]
    gate_ref, up_ref, gs_ref, us_ref, gain_ref, hid_ref = refs[18:]
    height = hid_ref.shape[0]
    width = 64 * 128
    units = gate_ref.shape[0]
    acc = jnp.zeros((height, 2 * units), F32)
    square = jnp.zeros((height, 128), F32)
    for r in range(8):
        for u in range(2):
            parts = []
            for chain in chains:
                a, a4, p, p4 = chain[0:4], chain[4], chain[5:8], chain[8]
                for m in range(4):
                    if r < 4:
                        parts.append(a[r][u, m])
                    elif r == 4:
                        parts.append(a4[m] if u == 0 else p4[(4 - m) % 4])
                    else:
                        parts.append(p[7 - r][1 - u, (4 - m) % 4])
            spans = column_spans(place_ref, chip_ahead(place_ref, 8 - r), u)
            x = jnp.concatenate(parts, axis=0).astype(F32)
            xx = x * x
            square = square + xx[:, 0:128] + xx[:, 128:256] + xx[:, 256:384] + xx[:, 384:512]
            gain = jnp.concatenate([gain_ref[:, s] for s in spans], axis=1)
            x = (x * gain).astype(BF)
            table = [jnp.concatenate([ref[:, s] for s in spans], axis=1) for ref in (gate_ref, up_ref)]
            acc = acc + dot_t(x, jnp.concatenate(table, axis=0))
    mean = jnp.sum(square, axis=1, keepdims=True) * (1.0 / width)
    norm = lax.rsqrt(mean + 1e-05) * (1.0 / (LEVEL * math.sqrt(width)))
    gate = acc[:, :units] * (norm * gs_ref[...].astype(F32))
    up = acc[:, units:] * (norm * us_ref[...].astype(F32))
    hid_ref[...] = (silu(gate) * up).astype(BF)


def down_kernel(place_ref, hid_ref, down_ref, scale_ref, *outs):
    half = hid_ref.shape[0] // 8
    fan = 64 * down_ref.shape[0]
    hid = hid_ref[...]
    for r in range(8):
        for u in range(2):
            spans = column_spans(place_ref, chip_ahead(place_ref, r), u)
            table = jnp.concatenate([down_ref[:, s] for s in spans], axis=1)
            scale = jnp.concatenate([scale_ref[:, s] for s in spans], axis=1)
            factor = scale.astype(F32) / (LEVEL * math.sqrt(fan))
            out = (dot(hid, table) * factor).astype(BF)
            back = (8 - r) % 8
            for h in range(2):
                mine, other, stay = outs[3 * h : 3 * h + 3]
                rows = [out[(4 * h + m) * half : (4 * h + m + 1) * half] for m in range(4)]
                for k in range(4):
                    if r == 0:
                        stay[u, k] = rows[(4 - k) % 4]
                    if 1 <= r < 4:
                        mine[(r - 1) * 2 + u, k] = rows[(4 - k) % 4]
                    if r == 4 and u == 0:
                        mine[6, k] = rows[(4 - k) % 4]
                    if r == 4 and u == 1:
                        other[6, k] = rows[k]
                    if r > 4:
                        other[(back - 1) * 2 + 1 - u, k] = rows[k]


def near_kernel(mine_ref, got_ref, come_ref, sum_ref):
    come = [come_ref[...], None] if len(come_ref.shape) == 3 else [come_ref[0], come_ref[1]]
    for u in range(2):
        total = add(mine_ref[u], got_ref[u])
        if come[u] is not None:
            total = total + come[u].astype(F32)
        sum_ref[u] = total.astype(BF)


def near_sum(mine, got, come, start):
    shape = (2,) + mine.shape[1:]
    zeros = (0,) * (len(shape) - 1)
    pair = pl.BlockSpec(shape, lambda i: (start // 2,) + zeros)
    return pl.pallas_call(
        near_kernel,
        out_shape=jax.ShapeDtypeStruct(shape, BF),
        grid=(1,),
        in_specs=[pair, pair, pl.BlockSpec(come.shape, lambda i: (0,) * come.ndim)],
        out_specs=pl.BlockSpec(shape, lambda i: (0,) + zeros),
        compiler_params=pltpu.CompilerParams(vmem_limit_bytes=8 * 1024 * 1024),
        cost_estimate=pl.CostEstimate(flops=0, bytes_accessed=0, transcendentals=0),
    )(mine, got, come)


def add(*parts):
    total = parts[0].astype(F32)
    for part in parts[1:]:
        total = total + part.astype(F32)
    return total


def sum_bf(*parts):
    return add(*parts).astype(BF)


def scatter_z(mine, other):
    got = swap_core(other)
    one = move_z(sum_bf(mine[6], got[6]))
    two = move_z(sum_bf(mine[5], got[5]))
    one, two = together(one, two)
    one = move_z(sum_bf(mine[4], got[4], one))
    two = move_z(sum_bf(mine[3], got[3], two))
    one, two = together(one, two)
    one = move_z(sum_bf(mine[2], got[2], one))
    two = move_z(sum_bf(mine[1], got[1], two))
    one, two = together(one, two)
    one = move_z(sum_bf(mine[0], got[0], one))
    return one, two


def on_device(
    mixer_input, gating_input, conv_cache, conv_weight, conv_bias, ssm_state, xproj_codes,
    xproj_scale, dtproj_codes, dtproj_scale, step_bias, decay_log, skip_gain, outproj_codes,
    outproj_scale, residual, norm_gain, expert_ids, expert_gates, gate_codes, up_codes,
    down_codes, gate_scale, up_scale, down_scale,
):
    rows, steps, slab = mixer_input.shape
    tokens = rows * steps
    group = tokens * 4
    model = outproj_codes.shape[-1]
    place = lax.axis_index("tensor")
    plane = lax.axis_index("expert")
    z, core = place // 2, place % 2
    where = jnp.stack([z, core, plane]).astype(jnp.int32)

    route = expert_ids.reshape(group, -1)
    gates = expert_gates.reshape(group, -1)
    capacity = 96
    half = capacity // 2
    slots = jnp.arange(capacity, dtype=jnp.int32)
    natural = jnp.arange(group, dtype=jnp.int32)
    held = natural
    held_token = (((plane + 4 - held // tokens) % 4) * rows + held % rows) * steps + (
        held % tokens
    ) // rows
    spread = (natural[:, None] == held_token[None, :]).astype(BF)
    hits = [jnp.any(route == (plane + m) % 4, axis=-1) for m in range(4)]
    members = jnp.stack(hits, axis=1).astype(jnp.int32)
    position = jnp.cumsum(members, axis=0, dtype=jnp.int32) - 1
    picks = jnp.stack(
        [
            (position[:, m][None, :] == slots[:, None]) & (members[:, m][None, :] == 1)
            for m in range(4)
        ]
    ).astype(BF)
    weight = jnp.sum(jnp.where(route == plane, gates, 0.0), axis=-1)
    slot_weight = jnp.sum(picks[0].astype(F32) * weight[None, :], axis=1)

    act, part = call(
        conv_kernel,
        (
            jax.ShapeDtypeStruct((steps, rows, slab), F32),
            jax.ShapeDtypeStruct((tokens, xproj_codes.shape[1]), F32),
        ),
        (
            mixer_input, conv_cache.transpose(1, 0, 2), conv_weight, conv_bias[None],
            xproj_codes.T,
        ),
        vmem_mib=56,
    )
    pair = part + swap_core(part)
    pair_bf = pair.astype(BF)
    prev, following = shift_z(pair_bf, 1), shift_z(pair_bf, -1)
    three = add(pair_bf, prev, following).astype(BF)
    two = add(pair_bf, prev).astype(BF)
    back, front = shift_z(three, 3), shift_z(two, -3)

    index = jnp.arange(slab, dtype=jnp.int32)
    column = ((plane + index // 128) % 4) * 128 + index % 128
    hadamard = sign_table(index[:, None], column[None, :], slab).astype(BF)
    rotated, new_state = call(
        scan_kernel,
        (
            jax.ShapeDtypeStruct((tokens, slab), BF),
            jax.ShapeDtypeStruct(ssm_state.shape, F32),
        ),
        (
            pair, prev, following, back, front, xproj_scale[None], dtproj_codes, dtproj_scale[None], step_bias[None],
            decay_log, act, gating_input, skip_gain[None], ssm_state, hadamard,
        ),
        scratch=(pltpu.VMEM((tokens, slab), F32), pltpu.VMEM((tokens, slab), F32)),
    )

    rotated = jnp.concatenate(
        [rotated[:, :128]] + [shift_y(rotated[:, m * 128 : (m + 1) * 128], m) for m in (1, 2, 3)]
    )
    other = swap_core(rotated)
    mine_f, other_f = rotated.astype(F32), other.astype(F32)
    paired = jnp.where(core == 0, mine_f + other_f, other_f - mine_f).astype(BF)
    prev, following = shift_z(paired, 1), shift_z(paired, -1)
    far = shift_z(jnp.concatenate([prev, paired, following]), -3)
    near = shift_z(jnp.concatenate([paired, following]), 3)
    signs = sign_table(z, (z + jnp.arange(8, dtype=jnp.int32)) % 8, 8)
    mine, others, stay = call(
        out_kernel,
        (
            jax.ShapeDtypeStruct((7, group, slab), BF),
            jax.ShapeDtypeStruct((7, group, slab), BF),
            jax.ShapeDtypeStruct((2, group, slab), BF),
        ),
        (
            signs, where, paired, following, prev, far, near, outproj_codes.reshape(128, model),
            outproj_scale[None],
        ),
        scalars=2,
    )

    one, two = scatter_z(mine, others)
    back = swap_core(sum_bf(stay[1], two))
    shares = call(
        route_kernel,
        jax.ShapeDtypeStruct((4, capacity + tokens, slab), BF),
        (where, stay, one, back, residual.reshape(group, 128), spread, picks),
        scalars=1,
        scratch=(pltpu.VMEM((group, slab), F32),),
    )
    hidden = sum_bf(shares[0], *[shift_y(shares[m], m) for m in (1, 2, 3)])
    slot_input = hidden[:capacity]
    hidden_here = jnp.concatenate([hidden[capacity:, i * 128 : (i + 1) * 128] for i in range(4)])

    up_x, down_x, far_x = (
        shift_x(slot_input, -1), shift_x(slot_input, 1), shift_x(slot_input, 2)
    )
    behind_x = jnp.where(core == 0, down_x, up_x)
    before_x = jnp.where(core == 0, up_x, down_x)
    mine = jnp.stack([slot_input, behind_x, far_x, before_x])
    back = swap_core(mine)
    tables = (gate_codes[0].T, up_codes[0].T, gate_scale, up_scale, norm_gain[None])
    carried = []
    for h in range(2):
        part, other = mine[:, h * half : (h + 1) * half], back[:, h * half : (h + 1) * half]
        carried.append([jnp.stack([part, jnp.stack([other[0], other[3], other[2], other[1]])])])
    starts = together(*[move_z(chain[-1]) for chain in carried])
    for chain, v in zip(carried, starts):
        chain.append(v)
    for _ in range(2):
        for chain in carried:
            chain.append(move_z(chain[-1]))
    for chain in carried:
        chain.append(move_z(chain[-1][0]))
    chains = [v for chain in carried for v in (*chain, *[swap_core(w) for w in chain[1:]])]
    height, units = 4 * capacity, gate_codes.shape[-1]
    hid = call(
        expert_kernel,
        jax.ShapeDtypeStruct((height, units), BF),
        (where, *chains, *tables),
        scalars=1,
        vmem_mib=24,
        flops=4 * height * units * model,
    )
    seven = jax.ShapeDtypeStruct((7, 4, half, slab), BF)
    two = jax.ShapeDtypeStruct((2, 4, half, slab), BF)
    down = call(
        down_kernel,
        (seven, seven, two, seven, seven, two),
        (where, hid, down_codes[0], down_scale),
        scalars=1,
        vmem_mib=20,
        flops=2 * height * units * model,
    )
    outs, gots, sums = [], [], []
    for mine, other, stay in (down[:3], down[3:]):
        got = swap_core(other)
        outs.append((mine, stay))
        gots.append(got)
        sums.append(move_z(sum_bf(mine[6], got[6])))
    sums = together(*sums)

    for start in (4, 2, 0):
        sums = [
            move_z(near_sum(out[0], got, v, start)) for out, got, v in zip(outs, gots, sums)
        ]
    ends = []
    for (_, stay), v in zip(outs, sums):
        back = sum_bf(stay[1], v[1])
        back = swap_core(jnp.stack([back[0], back[3], back[2], back[1]]))
        ends.append(sum_bf(stay[0], v[0], back))
    total = jnp.concatenate(ends, axis=1)
    expert_out = add(
        total[0], move_x(total[1]), move_x(total[3], -1), shift_x(total[2], 2)
    )
    expert_out = expert_out * slot_weight[:, None]
    expert_out = expert_out.astype(BF)

    moe = hidden_here.astype(F32)
    for m in range(4):
        part = lax.dynamic_slice_in_dim(expert_out, ((plane + 4 - m) % 4) * 128, 128, 1)
        if m:
            part = shift_y(part, 4 - m)
        moe = moe + dot(picks[m].T, part)
    return moe.astype(BF).reshape(rows * 4, steps, 128), new_state


def solution(mesh):
    rows = P(("dp", "expert"), None, "tensor")
    share = P("dp", None, ("expert", "tensor"))
    units = P("expert", None, ("dp", "tensor"))
    placed = (
        rows, rows, rows, P(None, "tensor"), P("tensor"), rows, P("tensor", None), P(),
        P(None, "tensor"), P("tensor"), P("tensor"), P(None, "tensor"), P("tensor"),
        P("tensor", "expert", None, None), P(), share, P(), P("dp", None, None),
        P("dp", None, None), units, units, P("expert", ("dp", "tensor"), None),
        P("expert", ("dp", "tensor")), P("expert", ("dp", "tensor")), P("expert", None),
    )
    return jax.shard_map(
        on_device, mesh=mesh, in_specs=placed, out_specs=(share, rows), check_vma=False
    )
```
